32 devices in a mesh: grp: 4 (over z), leaf: 8 (over y, x, core).
Axes of the slice: x: 2, y: 2, z: 4, core: 2. Of those that a mesh axis runs over, the one named last changes fastest.
Arguments:
- matrix: bfloat16 [32768, 512], P(('grp', 'leaf')), may hold values from -6 to 6
- leaf_basis: bfloat16 [32768, 512], P(('grp', 'leaf')), may hold values from -0.1875 to 0.1875
- leaf_tri: bfloat16 [32, 512, 512], P(('grp', 'leaf')), may hold values from -1.5 to 1.5, as said below
- inner_basis: bfloat16 [4, 8, 3, 1024, 512], P('grp', 'leaf'), may hold values from -1 to 1, as said below
- inner_tri: bfloat16 [4, 8, 3, 512, 512], P('grp', 'leaf'), may hold values from -1.5 to 1.5, as said below
- outer_basis: bfloat16 [4, 8, 2, 1024, 512], P('grp', 'leaf'), may hold values from -1 to 1, as said below
- outer_tri: bfloat16 [4, 8, 2, 512, 512], P('grp', 'leaf'), may hold values from -1.5 to 1.5, as said below
Outputs:
- reduced: bfloat16 [512, 512], P(None, ('grp', 'leaf'))
The draws below stay inside these ranges and needn't reach their ends.
Inputs may be any that keep to these rules, and one draw needn't show every extreme that they name: `leaf_tri`: upper triangular; diagonal entries between 0.5 and 1.5. `inner_basis`: equal for all leaves under the same inner node of level l. `inner_tri`: upper triangular, diagonal entries between 0.5 and 1.5; equal for all leaves under the same inner node of level l. `outer_basis`: equal for all leaves under the same outer node of level m. `outer_tri`: upper triangular, diagonal entries between 0.5 and 1.5; equal for all leaves under the same outer node of level m.
All inputs are finite; a program needn't handle non-finite values.
Results may differ from the reference program's by a relative error of at most 0.0045.
Values sent between devices are 32-bit elements; how exact they have to be, the bound alone decides.
A program may use at most 64 MiB of HBM per device.

```python
import jax
import jax.numpy as jnp
from jax import lax

K = 512
P_SIZE = 512
LEAF_ROWS = 1024
LEAF_DEPTH = 3
GRP_DEPTH = 2
ROWS = 32768
N_GRP = 4
N_LEAF = 8


def rough_values(first_key, shape):
    values = jnp.clip(jax.random.normal(first_key, shape, jnp.float32), -4.0, 4.0)
    return values


def triangle_table(first_key, leading):
    upper_key, diag_key = jax.random.split(first_key)
    upper = rough_values(upper_key, leading + (K, K)) * (0.5 / K ** 0.5)
    diagonal = jax.random.uniform(diag_key, leading + (K,), jnp.float32, 0.5, 1.5)
    strict = jnp.triu(jnp.ones((K, K), jnp.float32), 1)
    return (upper * strict + diagonal[..., None] * jnp.eye(K, dtype=jnp.float32)).astype(jnp.bfloat16)


def basis_table(first_key, leading):
    return (rough_values(first_key, leading + (2 * K, K)) * (2 * K) ** (-0.5)).astype(jnp.bfloat16)


def inner_nodes():
    leaf_ids = jnp.arange(N_LEAF, dtype=jnp.int32)[:, None]
    heights = jnp.arange(LEAF_DEPTH, dtype=jnp.int32)[None, :]
    return (heights, jnp.right_shift(leaf_ids, heights + 1))


def outer_nodes():
    group_ids = jnp.arange(N_GRP, dtype=jnp.int32)[:, None]
    heights = jnp.arange(GRP_DEPTH, dtype=jnp.int32)[None, :]
    return (heights, jnp.right_shift(group_ids, heights + 1))


def draw_leaf_tri(key, part):
    return triangle_table(jax.random.fold_in(key, 11), (N_GRP * N_LEAF,))


def draw_inner_basis(key, part):
    table = basis_table(jax.random.fold_in(key, 21), (N_GRP, LEAF_DEPTH, N_LEAF // 2))
    heights, node_ids = inner_nodes()
    return table[:, heights, node_ids]


def draw_inner_tri(key, part):
    table = triangle_table(jax.random.fold_in(key, 31), (N_GRP, LEAF_DEPTH, N_LEAF // 2))
    heights, node_ids = inner_nodes()
    return table[:, heights, node_ids]


def draw_outer_basis(key, part):
    table = basis_table(jax.random.fold_in(key, 41), (GRP_DEPTH, N_GRP // 2))
    heights, node_ids = outer_nodes()
    picked = table[heights, node_ids]
    return jnp.broadcast_to(picked[:, None], (N_GRP, N_LEAF, GRP_DEPTH, 2 * K, K))


def draw_outer_tri(key, part):
    table = triangle_table(jax.random.fold_in(key, 51), (GRP_DEPTH, N_GRP // 2))
    heights, node_ids = outer_nodes()
    picked = table[heights, node_ids]
    return jnp.broadcast_to(picked[:, None], (N_GRP, N_LEAF, GRP_DEPTH, K, K))


def levels(stream_key, dims, pieces, least, largest):
    loudness = 1.0
    for axis_at, blocks in pieces:
        steps = jax.random.uniform(jax.random.fold_in(jax.random.fold_in(stream_key, 6), axis_at), (blocks,), jnp.float32, least / len(pieces), largest / len(pieces))
        loudness = loudness * jnp.repeat(jnp.exp(steps), dims[axis_at] // blocks).reshape((-1,) + (1,) * (len(dims) - 1 - axis_at))
    return loudness


def noise(key, extent, deviation, most, shards=(), kind=jnp.bfloat16):
    drawn = deviation * jax.random.normal(key, extent, jnp.float32)
    if shards:
        drawn = drawn * levels(key, extent, shards, -0.22, 0.18)
    return jnp.clip(drawn, -most, most).astype(kind)


def setup_inputs(seed: int = 0) -> dict:
    streams_of = jax.random.split(jax.random.key(seed), 8)
    matrix = noise(streams_of[0], (ROWS, P_SIZE), 1.0, 6.0, ((0, 32),))
    leaf_basis = noise(streams_of[1], (ROWS, K), LEAF_ROWS ** -0.5, 0.1875, ((0, 32),))
    leaf_tri = draw_leaf_tri(jax.random.fold_in(streams_of[7], 71), 0)
    inner_basis = draw_inner_basis(jax.random.fold_in(streams_of[7], 71), 0)
    inner_tri = draw_inner_tri(jax.random.fold_in(streams_of[7], 71), 0)
    outer_basis = draw_outer_basis(jax.random.fold_in(streams_of[7], 71), 0)
    outer_tri = draw_outer_tri(jax.random.fold_in(streams_of[7], 71), 0)
    return {"matrix": matrix, "leaf_basis": leaf_basis, "leaf_tri": leaf_tri, "inner_basis": inner_basis, "inner_tri": inner_tri, "outer_basis": outer_basis, "outer_tri": outer_tri}


def leaf_reflect(panel_rows, reflectors, triangle):
    rank_width = triangle.shape[-1]
    projected = jnp.dot(reflectors.T, panel_rows, preferred_element_type=jnp.float32)
    mixing = jnp.dot(triangle.astype(jnp.float32).T, projected, precision=lax.Precision.HIGHEST)
    return panel_rows[:rank_width].astype(jnp.float32) - jnp.dot(reflectors[:rank_width].astype(jnp.float32), mixing, precision=lax.Precision.HIGHEST)


def node_reflect(panel_rows, reflectors, triangle):
    rank_width = triangle.shape[-1]
    basis = reflectors.astype(jnp.float32)
    projected = jnp.dot(basis.T, panel_rows, precision=lax.Precision.HIGHEST)
    mixing = jnp.dot(triangle.astype(jnp.float32).T, projected, precision=lax.Precision.HIGHEST)
    return panel_rows[:rank_width] - jnp.dot(basis[:rank_width], mixing, precision=lax.Precision.HIGHEST)


def leaf_tuple(packed):
    return leaf_reflect(packed[0], packed[1], packed[2])


def node_tuple(packed):
    return node_reflect(packed[0], packed[1], packed[2])


def reference(matrix, leaf_basis, leaf_tri, inner_basis, inner_tri, outer_basis, outer_tri):
    count_leaves = N_GRP * N_LEAF
    blocks = matrix.reshape(count_leaves, LEAF_ROWS, P_SIZE)
    leaf_bases = leaf_basis.reshape(count_leaves, LEAF_ROWS, K)
    summits = lax.map(leaf_tuple, (blocks, leaf_bases, leaf_tri))
    summits = summits.reshape(N_GRP, N_LEAF, K, P_SIZE)
    for height in range(LEAF_DEPTH):
        stride = 2 ** (height + 1)
        stacked = summits.reshape(N_GRP * (summits.shape[1] // 2), 2 * K, P_SIZE)
        node_basis = inner_basis[:, ::stride, height].reshape(-1, 2 * K, K)
        node_tri = inner_tri[:, ::stride, height].reshape(-1, K, K)
        summits = lax.map(node_tuple, (stacked, node_basis, node_tri)).reshape(N_GRP, -1, K, P_SIZE)
    summits = summits.reshape(N_GRP, K, P_SIZE)
    for height in range(GRP_DEPTH):
        stride = 2 ** (height + 1)
        stacked = summits.reshape(-1, 2 * K, P_SIZE)
        node_basis = outer_basis[::stride, 0, height]
        node_tri = outer_tri[::stride, 0, height]
        summits = lax.map(node_tuple, (stacked, node_basis, node_tri))
    return summits[0].astype(jnp.bfloat16)
```

```python
import functools

import jax
import jax.numpy as jnp
from jax import lax
from jax.experimental import pallas as pl
from jax.experimental.pallas import tpu as pltpu
from jax.sharding import PartitionSpec as P

MESH = pl.DeviceIdType.MESH
F32 = jnp.float32
BF16 = jnp.bfloat16


def dot(left, right):
    return jnp.dot(left, right, preferred_element_type=F32)


def dot_nt(left, right):
    return lax.dot_general(left, right, (((1,), (1,)), ((), ())), preferred_element_type=F32)


def twice(values, product, weights):
    count = values.shape[0]
    high = values.astype(BF16)
    low = (values - high.astype(F32)).astype(BF16)
    both = product(jnp.concatenate([high, low], axis=0), weights)
    return both[:count] + both[count:]


def bit_of(index, height):
    return lax.rem(lax.div(index, 2**height), 2)


def flipped(index, mask):
    for height in range(mask.bit_length()):
        if mask >> height & 1:
            index = index + 2**height * (1 - 2 * bit_of(index, height))
    return index


def reversed_bits(index, count):
    return sum((index >> i & 1) << (count - 1 - i) for i in range(count))


def plan(panel, n_leaf, n_grp):
    inner_rows = panel // n_leaf
    return inner_rows, inner_rows // n_grp >= 8


def axis_orders(bits):
    half = (len(bits) + 1) // 2
    return (bits, bits[half:] + bits[:half])


def kernel(n_leaf, n_grp, *refs):
    (matrix, leaf_basis, leaf_tri, inner_basis, inner_tri, outer_basis, outer_tri, out,
     panel_v, leaf_v, leaf_f, node_v, node_f, first, kept, first_in, parts, parts_in,
     last, last_in, load_sem, send_sem, recv_sem) = refs
    panel = matrix.shape[1]
    k = leaf_tri.shape[-1]
    inner, outer = n_leaf.bit_length() - 1, n_grp.bit_length() - 1
    inner_rows, scatter = plan(panel, n_leaf, n_grp)
    leaf, grp = lax.axis_index("leaf"), lax.axis_index("grp")

    barrier = pltpu.get_barrier_semaphore()
    for height in range(inner):
        pl.semaphore_signal(barrier, inc=1, device_id={"leaf": flipped(leaf, 1 << height)}, device_id_type=MESH)
    for mask in range(1, n_grp):
        pl.semaphore_signal(barrier, inc=1, device_id={"grp": flipped(grp, mask)}, device_id_type=MESH)

    pairs = [(matrix, panel_v), (leaf_basis, leaf_v), (leaf_tri.at[0], leaf_f)]
    for height in range(inner):
        pairs.append((inner_basis.at[0, 0, height], node_v.at[height]))
        pairs.append((inner_tri.at[0, 0, height], node_f.at[height]))
    for height in range(outer):
        pairs.append((outer_basis.at[0, 0, height], node_v.at[inner + height]))
        pairs.append((outer_tri.at[0, 0, height], node_f.at[inner + height]))
    loads = [pltpu.make_async_copy(src, dst, load_sem.at[i]) for i, (src, dst) in enumerate(pairs)]
    for load in loads:
        load.start()

    sent = []

    def send(src, dst, device):
        slot = len(sent)
        copy = pltpu.make_async_remote_copy(
            src_ref=src, dst_ref=dst, send_sem=send_sem.at[slot], recv_sem=recv_sem.at[slot],
            device_id=device, device_id_type=MESH)
        copy.start()
        sent.append(copy)
        return copy

    columns = lax.broadcasted_iota(jnp.int32, (1, panel), 1)
    width = panel // (n_leaf * n_grp)
    owner, target = lax.div(columns, width), lax.rem(columns, width)
    for height in range(inner + outer):
        bit = bit_of(owner, height)
        if height < inner or scatter:
            mine = bit_of(leaf, height) if height < inner else bit_of(grp, height - inner)
            target = target + (bit + mine - 2 * bit * mine) * (panel >> (height + 1))
        else:
            target = target + bit * (width << (height - inner))

    half = panel // 2

    def leaf_rows(start):
        rows = lax.broadcasted_iota(jnp.int32, (half, panel), 0) + start
        order = jnp.where(rows == target, 1.0, 0.0).astype(BF16)
        turned = dot_nt(order, panel_v[...]).astype(BF16)
        mixing = twice(dot(turned, leaf_v[...]), dot, leaf_f[...])
        return turned[:, :k].astype(F32) - twice(mixing, dot_nt, leaf_v[:k, :])

    for load in loads[:3]:
        load.wait()
    first[...] = leaf_rows(half)
    pl.semaphore_wait(barrier, inner + n_grp - 1)
    arriving = send(first, first_in, {"leaf": flipped(leaf, 1)})
    kept[...] = leaf_rows(0)

    def load_node(level):
        loads[3 + 2 * level].wait()
        loads[4 + 2 * level].wait()

    def half_basis(level, parity):
        return node_v[level, pl.ds(pl.multiple_of(parity * k, k), k), :]

    load_node(0)
    parity = bit_of(leaf, 0)
    projected = twice(kept[...], dot, half_basis(0, parity))
    arriving.wait_recv()
    projected = projected + twice(first_in[...], dot, half_basis(0, 1 - parity))
    mixing = twice(projected, dot, node_f[0])
    summit = jnp.where(parity == 0, kept[...], first_in[...]) - twice(mixing, dot_nt, node_v[0, :k, :])

    def own_mixing(summit, level, parity):
        projected = twice(summit, dot, half_basis(level, parity))
        return twice(projected, dot, node_f[level]), jnp.where(parity == 0, summit, 0.0)

    for level in range(1, inner - 1):
        load_node(level)
        mixing, top = own_mixing(summit, level, bit_of(leaf, level))
        summit = top - twice(mixing, dot_nt, node_v[level, :k, :])
    level = inner - 1
    load_node(level)
    mixing, top = own_mixing(summit, level, bit_of(leaf, level))

    bits = tuple(range(1, inner))
    orders = axis_orders(bits)
    lanes = k // 2
    left = [list(bits) for _ in orders]
    waiting = [None, None]

    def pick(group, height, side):
        return (slice(None),) * left[group].index(height) + (side,)

    def send_part(group, step):
        height = orders[group][step]
        waiting[group] = send(
            parts[group][step].at[pick(group, height, 1)], parts_in[group][step],
            {"leaf": flipped(leaf, 1 << height)})

    for group in range(2):
        span = slice(group * lanes, (group + 1) * lanes)
        term = top[:, span] - twice(mixing, dot_nt, node_v[level, span, :])
        parts[group][0][...] = term.reshape(parts[group][0].shape)
        send_part(group, 0)
    sums = [None, None]
    for step in range(len(bits)):
        for group in range(2):
            height = orders[group][step]
            waiting[group].wait_recv()
            total = parts[group][step][pick(group, height, 0)] + parts_in[group][step][...]
            left[group].remove(height)
            if step + 1 < len(bits):
                parts[group][step + 1][...] = total
                send_part(group, step + 1)
            else:
                sums[group] = total
    summit = jnp.concatenate(sums, axis=1)

    for height in range(outer):
        load_node(inner + height)
        mixing, top = own_mixing(summit, inner + height, bit_of(grp, height))
        summit = top - twice(mixing, dot_nt, node_v[inner + height, :k, :])
    last[...] = summit.reshape(last.shape)
    coming = []
    for mask in range(1, n_grp):
        piece = reversed_bits(mask, outer) if scatter else 0
        coming.append(send(last.at[piece], last_in.at[mask - 1], {"grp": flipped(grp, mask)}))
    total = last[0]
    for slot, copy in enumerate(coming):
        copy.wait_recv()
        total = total + last_in[slot]
    out[...] = total.astype(out.dtype)
    for copy in sent:
        copy.wait_send()


def per_device(matrix, leaf_basis, leaf_tri, inner_basis, inner_tri, outer_basis, outer_tri):
    n_leaf, n_grp = lax.axis_size("leaf"), lax.axis_size("grp")
    panel, k = matrix.shape[1], leaf_tri.shape[-1]
    inner, outer = n_leaf.bit_length() - 1, n_grp.bit_length() - 1
    inner_rows, scatter = plan(panel, n_leaf, n_grp)
    levels = inner + outer
    rows = inner_rows // n_grp if scatter else inner_rows
    half = panel // 2
    lead = lambda count: (2,) * count + (inner_rows, k // 2)
    parts = [[pltpu.VMEM(lead(inner - 1 - s), F32) for s in range(inner - 1)] for _ in range(2)]
    parts_in = [[pltpu.VMEM(lead(inner - 2 - s), F32) for s in range(inner - 1)] for _ in range(2)]
    copies = 1 + 2 * (inner - 1) + n_grp - 1
    result = pl.pallas_call(
        functools.partial(kernel, n_leaf, n_grp),
        out_shape=jax.ShapeDtypeStruct((rows, k), BF16),
        in_specs=[pl.BlockSpec(memory_space=pl.ANY)] * 7,
        out_specs=pl.BlockSpec(memory_space=pltpu.VMEM),
        scratch_shapes=[
            pltpu.VMEM(matrix.shape, BF16),
            pltpu.VMEM(leaf_basis.shape, BF16),
            pltpu.VMEM(leaf_tri.shape[1:], BF16),
            pltpu.VMEM((levels,) + inner_basis.shape[-2:], BF16),
            pltpu.VMEM((levels,) + inner_tri.shape[-2:], BF16),
            pltpu.VMEM((half, k), F32),
            pltpu.VMEM((half, k), F32),
            pltpu.VMEM((half, k), F32),
            parts,
            parts_in,
            pltpu.VMEM((n_grp if scatter else 1, rows, k), F32),
            pltpu.VMEM((n_grp - 1, rows, k), F32),
            pltpu.SemaphoreType.DMA((3 + 2 * levels,)),
            pltpu.SemaphoreType.DMA((copies,)),
            pltpu.SemaphoreType.DMA((copies,)),
        ],
        compiler_params=pltpu.CompilerParams(
            collective_id=0, has_side_effects=True, vmem_limit_bytes=60 * 2**20),
        cost_estimate=pl.CostEstimate(flops=30 * 2 * k**3, bytes_accessed=10 * 2**20, transcendentals=0),
    )(matrix, leaf_basis, leaf_tri, inner_basis, inner_tri, outer_basis, outer_tri)
    if not scatter:
        width = panel // (n_leaf * n_grp)
        result = lax.dynamic_slice_in_dim(result, lax.axis_index("grp") * width, width, 0)
    return result.T


def solution(mesh):
    placed = (
        P(("grp", "leaf"), None),
        P(("grp", "leaf"), None),
        P(("grp", "leaf"), None, None),
        P("grp", "leaf", None, None, None),
        P("grp", "leaf", None, None, None),
        P("grp", "leaf", None, None, None),
        P("grp", "leaf", None, None, None),
    )
    return jax.shard_map(
        per_device, mesh=mesh, in_specs=placed, out_specs=P(None, ("grp", "leaf")), check_vma=False
    )
```

```python
import functools

import jax
import jax.numpy as jnp
from jax import lax
from jax.experimental import pallas as pl
from jax.experimental.pallas import tpu as pltpu
from jax.sharding import PartitionSpec as P

MESH = pl.DeviceIdType.MESH
F32 = jnp.float32
BF16 = jnp.bfloat16
STREAMS = 2


def dot(left, right):
    return jnp.dot(left, right, preferred_element_type=F32)


def dot_nt(left, right):
    return lax.dot_general(left, right, (((1,), (1,)), ((), ())), preferred_element_type=F32)


def twice(values, product, weights):
    count = values.shape[0]
    high = values.astype(BF16).astype(F32)
    both = product(jnp.concatenate([high, values - high], axis=0).astype(BF16), weights)
    return both[:count] + both[count:]


def bit_of(index, height):
    return lax.rem(lax.div(index, 2**height), 2)


def flipped(index, mask):
    for height in range(mask.bit_length()):
        if mask >> height & 1:
            index = index + 2**height * (1 - 2 * bit_of(index, height))
    return index


def reversed_bits(index, count):
    return sum((index >> i & 1) << (count - 1 - i) for i in range(count))


def plan(panel, n_leaf, n_grp):
    inner_rows = panel // n_leaf // STREAMS
    return inner_rows, inner_rows // n_grp >= 8


def axis_orders(bits):
    half = (len(bits) + 1) // 2
    return (bits, bits[half:] + bits[:half])


def kernel(n_leaf, n_grp, *refs):
    (matrix, leaf_basis, leaf_tri, inner_basis, inner_tri, outer_basis, outer_tri, out,
     panel_v, leaf_v, leaf_f, node_v, node_f, first, kept, first_in, parts, parts_in,
     last, last_in, load_sem, send_sem, recv_sem) = refs
    panel = matrix.shape[1]
    k = leaf_tri.shape[-1]
    inner, outer = n_leaf.bit_length() - 1, n_grp.bit_length() - 1
    inner_rows, scatter = plan(panel, n_leaf, n_grp)
    leaf, grp = lax.axis_index("leaf"), lax.axis_index("grp")

    barrier = pltpu.get_barrier_semaphore()
    for height in range(inner):
        pl.semaphore_signal(barrier, inc=1, device_id={"leaf": flipped(leaf, 1 << height)}, device_id_type=MESH)
    for mask in range(1, n_grp):
        pl.semaphore_signal(barrier, inc=1, device_id={"grp": flipped(grp, mask)}, device_id_type=MESH)

    pairs = [(matrix, panel_v), (leaf_basis, leaf_v), (leaf_tri.at[0], leaf_f)]
    for height in range(inner):
        pairs.append((inner_basis.at[0, 0, height], node_v.at[height]))
        pairs.append((inner_tri.at[0, 0, height], node_f.at[height]))
    for height in range(outer):
        pairs.append((outer_basis.at[0, 0, height], node_v.at[inner + height]))
        pairs.append((outer_tri.at[0, 0, height], node_f.at[inner + height]))
    loads = [pltpu.make_async_copy(src, dst, load_sem.at[i]) for i, (src, dst) in enumerate(pairs)]
    for load in loads:
        load.start()

    sent = []

    def send(src, dst, device):
        slot = len(sent)
        copy = pltpu.make_async_remote_copy(
            src_ref=src, dst_ref=dst, send_sem=send_sem.at[slot], recv_sem=recv_sem.at[slot],
            device_id=device, device_id_type=MESH)
        copy.start()
        sent.append(copy)
        return copy

    columns = lax.broadcasted_iota(jnp.int32, (1, panel), 1)
    stream_rows = panel // STREAMS
    width = panel // (n_leaf * n_grp)
    narrow = width // STREAMS
    owner, place = lax.div(columns, width), lax.rem(columns, width)
    target = lax.div(place, narrow) * stream_rows + lax.rem(place, narrow)
    for height in range(inner + outer):
        bit = bit_of(owner, height)
        if height < inner or scatter:
            mine = bit_of(leaf, height) if height < inner else bit_of(grp, height - inner)
            target = target + (bit + mine - 2 * bit * mine) * (stream_rows >> (height + 1))
        else:
            target = target + bit * (narrow << (height - inner))

    half = stream_rows // 2
    streams = range(STREAMS)

    def leaf_rows(stream):
        rows = lax.broadcasted_iota(jnp.int32, (stream_rows, panel), 0) + stream * stream_rows
        order = jnp.where(rows == target, 1.0, 0.0).astype(BF16)
        turned = dot_nt(order, panel_v[...]).astype(BF16)
        mixing = twice(dot(turned, leaf_v[...]), dot, leaf_f[...])
        return turned[:, :k].astype(F32) - twice(mixing, dot_nt, leaf_v[:k, :])

    def load_node(level):
        loads[3 + 2 * level].wait()
        loads[4 + 2 * level].wait()

    def half_basis(level, parity):
        return node_v[level, pl.ds(pl.multiple_of(parity * k, k), k), :]

    for load in loads[:3]:
        load.wait()
    arriving = []
    for stream in streams:
        summit = leaf_rows(stream)
        kept[stream] = summit[:half]
        first[stream] = summit[half:]
        if stream == 0:
            pl.semaphore_wait(barrier, inner + n_grp - 1)
        arriving.append(send(first.at[stream], first_in.at[stream], {"leaf": flipped(leaf, 1)}))

    def own_mixing(summit, level, parity):
        projected = twice(summit, dot, half_basis(level, parity))
        return twice(projected, dot, node_f[level]), jnp.where(parity == 0, summit, 0.0)

    bits = tuple(range(1, inner))
    orders = axis_orders(bits)
    lanes = k // 2
    left = [[list(bits) for _ in orders] for _ in streams]
    waiting = [[None, None] for _ in streams]

    def pick(stream, group, height, side):
        return (slice(None),) * left[stream][group].index(height) + (side,)

    def send_part(stream, group, step):
        height = orders[group][step]
        waiting[stream][group] = send(
            parts[stream][group][step].at[pick(stream, group, height, 1)], parts_in[stream][group][step],
            {"leaf": flipped(leaf, 1 << height)})

    for level in range(inner):
        load_node(level)
    for stream in streams:
        parity = bit_of(leaf, 0)
        projected = twice(kept[stream], dot, half_basis(0, parity))
        arriving[stream].wait_recv()
        projected = projected + twice(first_in[stream], dot, half_basis(0, 1 - parity))
        mixing = twice(projected, dot, node_f[0])
        top = jnp.where(parity == 0, kept[stream], first_in[stream])
        summit = top - twice(mixing, dot_nt, node_v[0, :k, :])
        for level in range(1, inner - 1):
            mixing, top = own_mixing(summit, level, bit_of(leaf, level))
            summit = top - twice(mixing, dot_nt, node_v[level, :k, :])
        level = inner - 1
        mixing, top = own_mixing(summit, level, bit_of(leaf, level))
        for group in range(2):
            span = slice(group * lanes, (group + 1) * lanes)
            term = top[:, span] - twice(mixing, dot_nt, node_v[level, span, :])
            parts[stream][group][0][...] = term.reshape(parts[stream][group][0].shape)
            send_part(stream, group, 0)

    for height in range(outer):
        load_node(inner + height)
    sums = [[None, None] for _ in streams]
    coming = [[] for _ in streams]
    for step in range(len(bits)):
        for stream in streams:
            for group in range(2):
                height = orders[group][step]
                waiting[stream][group].wait_recv()
                total = parts[stream][group][step][pick(stream, group, height, 0)] + parts_in[stream][group][step][...]
                left[stream][group].remove(height)
                if step + 1 < len(bits):
                    parts[stream][group][step + 1][...] = total
                    send_part(stream, group, step + 1)
                else:
                    sums[stream][group] = total
            if step + 1 == len(bits):
                summit = jnp.concatenate(sums[stream], axis=1)
                for height in range(outer):
                    mixing, top = own_mixing(summit, inner + height, bit_of(grp, height))
                    summit = top - twice(mixing, dot_nt, node_v[inner + height, :k, :])
                last[stream] = summit.reshape(last.shape[1:])
                for mask in range(1, n_grp):
                    piece = reversed_bits(mask, outer) if scatter else 0
                    coming[stream].append(send(
                        last.at[stream, piece], last_in.at[stream, mask - 1], {"grp": flipped(grp, mask)}))
    totals = []
    for stream in streams:
        total = last[stream, 0]
        for slot, copy in enumerate(coming[stream]):
            copy.wait_recv()
            total = total + last_in[stream, slot]
        totals.append(total)
    out[...] = jnp.concatenate(totals, axis=0).astype(out.dtype)
    for copy in sent:
        copy.wait_send()


def per_device(matrix, leaf_basis, leaf_tri, inner_basis, inner_tri, outer_basis, outer_tri):
    n_leaf, n_grp = lax.axis_size("leaf"), lax.axis_size("grp")
    panel, k = matrix.shape[1], leaf_tri.shape[-1]
    inner, outer = n_leaf.bit_length() - 1, n_grp.bit_length() - 1
    inner_rows, scatter = plan(panel, n_leaf, n_grp)
    levels = inner + outer
    rows = inner_rows // n_grp if scatter else inner_rows
    half = panel // STREAMS // 2
    lead = lambda count: (2,) * count + (inner_rows, k // 2)
    steps = range(inner - 1)
    parts = [[[pltpu.VMEM(lead(inner - 1 - s), F32) for s in steps] for _ in range(2)] for _ in range(STREAMS)]
    parts_in = [[[pltpu.VMEM(lead(inner - 2 - s), F32) for s in steps] for _ in range(2)] for _ in range(STREAMS)]
    copies = STREAMS * (1 + 2 * (inner - 1) + n_grp - 1)
    result = pl.pallas_call(
        functools.partial(kernel, n_leaf, n_grp),
        out_shape=jax.ShapeDtypeStruct((STREAMS * rows, k), BF16),
        in_specs=[pl.BlockSpec(memory_space=pl.ANY)] * 7,
        out_specs=pl.BlockSpec(memory_space=pltpu.VMEM),
        scratch_shapes=[
            pltpu.VMEM(matrix.shape, BF16),
            pltpu.VMEM(leaf_basis.shape, BF16),
            pltpu.VMEM(leaf_tri.shape[1:], BF16),
            pltpu.VMEM((levels,) + inner_basis.shape[-2:], BF16),
            pltpu.VMEM((levels,) + inner_tri.shape[-2:], BF16),
            pltpu.VMEM((STREAMS, half, k), F32),
            pltpu.VMEM((STREAMS, half, k), F32),
            pltpu.VMEM((STREAMS, half, k), F32),
            parts,
            parts_in,
            pltpu.VMEM((STREAMS, n_grp if scatter else 1, rows, k), F32),
            pltpu.VMEM((STREAMS, n_grp - 1, rows, k), F32),
            pltpu.SemaphoreType.DMA((3 + 2 * levels,)),
            pltpu.SemaphoreType.DMA((copies,)),
            pltpu.SemaphoreType.DMA((copies,)),
        ],
        compiler_params=pltpu.CompilerParams(
            collective_id=0, has_side_effects=True, vmem_limit_bytes=60 * 2**20),
        cost_estimate=pl.CostEstimate(flops=30 * 2 * k**3, bytes_accessed=10 * 2**20, transcendentals=0),
    )(matrix, leaf_basis, leaf_tri, inner_basis, inner_tri, outer_basis, outer_tri)
    if not scatter:
        narrow = panel // (n_leaf * n_grp) // STREAMS
        result = result.reshape(STREAMS, rows, k)
        result = lax.dynamic_slice_in_dim(result, lax.axis_index("grp") * narrow, narrow, 1)
        result = result.reshape(STREAMS * narrow, k)
    return result.T


def solution(mesh):
    placed = (
        P(("grp", "leaf"), None),
        P(("grp", "leaf"), None),
        P(("grp", "leaf"), None, None),
        P("grp", "leaf", None, None, None),
        P("grp", "leaf", None, None, None),
        P("grp", "leaf", None, None, None),
        P("grp", "leaf", None, None, None),
    )
    return jax.shard_map(
        per_device, mesh=mesh, in_specs=placed, out_specs=P(None, ("grp", "leaf")), check_vma=False
    )
```

```python
import functools

import jax
import jax.numpy as jnp
from jax import lax
from jax.experimental import pallas as pl
from jax.experimental.pallas import tpu as pltpu
from jax.sharding import PartitionSpec as P

MESH = pl.DeviceIdType.MESH
F32 = jnp.float32
BF16 = jnp.bfloat16
STREAMS = 2


def dot(left, right):
    return jnp.dot(left, right, preferred_element_type=F32)


def dot_nt(left, right):
    return lax.dot_general(left, right, (((1,), (1,)), ((), ())), preferred_element_type=F32)


def twice(values, product, weights):
    count = values.shape[0]
    high = values.astype(BF16).astype(F32)
    if count >= 128:
        return product(high.astype(BF16), weights) + product((values - high).astype(BF16), weights)
    both = product(jnp.concatenate([high, values - high], axis=0).astype(BF16), weights)
    return both[:count] + both[count:]


def bit_of(index, height):
    return lax.rem(lax.div(index, 2**height), 2)


def flipped(index, mask):
    for height in range(mask.bit_length()):
        if mask >> height & 1:
            index = index + 2**height * (1 - 2 * bit_of(index, height))
    return index


def reversed_bits(index, count):
    return sum((index >> i & 1) << (count - 1 - i) for i in range(count))


def plan(panel, n_leaf, n_grp):
    inner_rows = panel // n_leaf // STREAMS
    return inner_rows, inner_rows // n_grp >= 8


def axis_orders(bits):
    half = (len(bits) + 1) // 2
    return (bits, bits[half:] + bits[:half])


def kernel(n_leaf, n_grp, *refs):
    (matrix, leaf_basis, leaf_tri, inner_basis, inner_tri, outer_basis, outer_tri, out,
     panel_v, leaf_v, leaf_f, node_v, node_f, first, kept, first_in, parts, parts_in,
     last, last_in, load_sem, send_sem, recv_sem) = refs
    panel = matrix.shape[1]
    k = leaf_tri.shape[-1]
    inner, outer = n_leaf.bit_length() - 1, n_grp.bit_length() - 1
    inner_rows, scatter = plan(panel, n_leaf, n_grp)
    leaf, grp = lax.axis_index("leaf"), lax.axis_index("grp")

    barrier = pltpu.get_barrier_semaphore()
    for height in range(inner):
        pl.semaphore_signal(barrier, inc=1, device_id={"leaf": flipped(leaf, 1 << height)}, device_id_type=MESH)
    for mask in range(1, n_grp):
        pl.semaphore_signal(barrier, inc=1, device_id={"grp": flipped(grp, mask)}, device_id_type=MESH)

    pairs = [(matrix, panel_v), (leaf_basis, leaf_v), (leaf_tri.at[0], leaf_f)]
    for height in range(inner):
        pairs.append((inner_basis.at[0, 0, height], node_v.at[height]))
        pairs.append((inner_tri.at[0, 0, height], node_f.at[height]))
    for height in range(outer):
        pairs.append((outer_basis.at[0, 0, height], node_v.at[inner + height]))
        pairs.append((outer_tri.at[0, 0, height], node_f.at[inner + height]))
    loads = [pltpu.make_async_copy(src, dst, load_sem.at[i]) for i, (src, dst) in enumerate(pairs)]
    for load in loads[:3]:
        load.start()

    sent = []

    def send(src, dst, device):
        slot = len(sent)
        copy = pltpu.make_async_remote_copy(
            src_ref=src, dst_ref=dst, send_sem=send_sem.at[slot], recv_sem=recv_sem.at[slot],
            device_id=device, device_id_type=MESH)
        copy.start()
        sent.append(copy)
        return copy

    columns = lax.broadcasted_iota(jnp.int32, (1, panel), 1)
    stream_rows = panel // STREAMS
    width = panel // (n_leaf * n_grp)
    narrow = width // STREAMS
    owner, place = lax.div(columns, width), lax.rem(columns, width)
    target = lax.div(place, narrow) * stream_rows + lax.rem(place, narrow)
    for height in range(inner + outer):
        bit = bit_of(owner, height)
        if height < inner or scatter:
            mine = bit_of(leaf, height) if height < inner else bit_of(grp, height - inner)
            target = target + (bit + mine - 2 * bit * mine) * (stream_rows >> (height + 1))
        else:
            target = target + bit * (narrow << (height - inner))

    half = stream_rows // 2
    streams = range(STREAMS)

    def leaf_rows(stream):
        rows = lax.broadcasted_iota(jnp.int32, (stream_rows, panel), 0) + stream * stream_rows
        order = jnp.where(rows == target, 1.0, 0.0).astype(BF16)
        turned = dot_nt(order, panel_v[...]).astype(BF16)
        mixing = twice(dot(turned, leaf_v[...]), dot, leaf_f[...])
        return turned[:, :k].astype(F32) - twice(mixing, dot_nt, leaf_v[:k, :])

    def load_node(level):
        loads[3 + 2 * level].wait()
        loads[4 + 2 * level].wait()

    def half_basis(level, parity):
        return node_v[level, pl.ds(pl.multiple_of(parity * k, k), k), :]

    for load in loads[:3]:
        load.wait()
    for load in loads[3:]:
        load.start()
    arriving = []
    for stream in streams:
        summit = leaf_rows(stream)
        kept[stream] = summit[:half]
        first[stream] = summit[half:]
        if stream == 0:
            pl.semaphore_wait(barrier, inner + n_grp - 1)
        arriving.append(send(first.at[stream], first_in.at[stream], {"leaf": flipped(leaf, 1)}))

    def own_mixing(summit, level, parity):
        projected = twice(summit, dot, half_basis(level, parity))
        return twice(projected, dot, node_f[level]), jnp.where(parity == 0, summit, 0.0)

    bits = tuple(range(1, inner))
    orders = axis_orders(bits)
    lanes = k // 2
    left = [[list(bits) for _ in orders] for _ in streams]
    waiting = [[None, None] for _ in streams]

    def pick(stream, group, height, side):
        return (slice(None),) * left[stream][group].index(height) + (side,)

    def send_part(stream, group, step):
        height = orders[group][step]
        waiting[stream][group] = send(
            parts[stream][group][step].at[pick(stream, group, height, 1)], parts_in[stream][group][step],
            {"leaf": flipped(leaf, 1 << height)})

    for level in range(inner):
        load_node(level)
    for stream in streams:
        parity = bit_of(leaf, 0)
        projected = twice(kept[stream], dot, half_basis(0, parity))
        arriving[stream].wait_recv()
        projected = projected + twice(first_in[stream], dot, half_basis(0, 1 - parity))
        mixing = twice(projected, dot, node_f[0])
        top = jnp.where(parity == 0, kept[stream], first_in[stream])
        summit = top - twice(mixing, dot_nt, node_v[0, :k, :])
        for level in range(1, inner - 1):
            mixing, top = own_mixing(summit, level, bit_of(leaf, level))
            summit = top - twice(mixing, dot_nt, node_v[level, :k, :])
        level = inner - 1
        mixing, top = own_mixing(summit, level, bit_of(leaf, level))
        for group in range(2):
            span = slice(group * lanes, (group + 1) * lanes)
            term = top[:, span] - twice(mixing, dot_nt, node_v[level, span, :])
            parts[stream][group][0][...] = term.reshape(parts[stream][group][0].shape)
            send_part(stream, group, 0)

    for height in range(outer):
        load_node(inner + height)
    sums = [[None, None] for _ in streams]
    coming = [[] for _ in streams]
    for step in range(len(bits)):
        for stream in streams:
            for group in range(2):
                height = orders[group][step]
                waiting[stream][group].wait_recv()
                total = parts[stream][group][step][pick(stream, group, height, 0)] + parts_in[stream][group][step][...]
                left[stream][group].remove(height)
                if step + 1 < len(bits):
                    parts[stream][group][step + 1][...] = total
                    send_part(stream, group, step + 1)
                else:
                    sums[stream][group] = total
            if step + 1 == len(bits):
                summit = jnp.concatenate(sums[stream], axis=1)
                for height in range(outer):
                    mixing, top = own_mixing(summit, inner + height, bit_of(grp, height))
                    summit = top - twice(mixing, dot_nt, node_v[inner + height, :k, :])
                last[stream] = summit.reshape(last.shape[1:])
                for mask in range(1, n_grp):
                    piece = reversed_bits(mask, outer) if scatter else 0
                    coming[stream].append(send(
                        last.at[stream, piece], last_in.at[stream, mask - 1], {"grp": flipped(grp, mask)}))
    totals = []
    for stream in streams:
        total = last[stream, 0]
        for slot, copy in enumerate(coming[stream]):
            copy.wait_recv()
            total = total + last_in[stream, slot]
        totals.append(total)
    out[...] = jnp.concatenate(totals, axis=0).astype(out.dtype)
    for copy in sent:
        copy.wait_send()


def per_device(matrix, leaf_basis, leaf_tri, inner_basis, inner_tri, outer_basis, outer_tri):
    n_leaf, n_grp = lax.axis_size("leaf"), lax.axis_size("grp")
    panel, k = matrix.shape[1], leaf_tri.shape[-1]
    inner, outer = n_leaf.bit_length() - 1, n_grp.bit_length() - 1
    inner_rows, scatter = plan(panel, n_leaf, n_grp)
    levels = inner + outer
    rows = inner_rows // n_grp if scatter else inner_rows
    half = panel // STREAMS // 2
    lead = lambda count: (2,) * count + (inner_rows, k // 2)
    steps = range(inner - 1)
    parts = [[[pltpu.VMEM(lead(inner - 1 - s), F32) for s in steps] for _ in range(2)] for _ in range(STREAMS)]
    parts_in = [[[pltpu.VMEM(lead(inner - 2 - s), F32) for s in steps] for _ in range(2)] for _ in range(STREAMS)]
    copies = STREAMS * (1 + 2 * (inner - 1) + n_grp - 1)
    result = pl.pallas_call(
        functools.partial(kernel, n_leaf, n_grp),
        out_shape=jax.ShapeDtypeStruct((STREAMS * rows, k), BF16),
        in_specs=[pl.BlockSpec(memory_space=pl.ANY)] * 7,
        out_specs=pl.BlockSpec(memory_space=pltpu.VMEM),
        scratch_shapes=[
            pltpu.VMEM(matrix.shape, BF16),
            pltpu.VMEM(leaf_basis.shape, BF16),
            pltpu.VMEM(leaf_tri.shape[1:], BF16),
            pltpu.VMEM((levels,) + inner_basis.shape[-2:], BF16),
            pltpu.VMEM((levels,) + inner_tri.shape[-2:], BF16),
            pltpu.VMEM((STREAMS, half, k), F32),
            pltpu.VMEM((STREAMS, half, k), F32),
            pltpu.VMEM((STREAMS, half, k), F32),
            parts,
            parts_in,
            pltpu.VMEM((STREAMS, n_grp if scatter else 1, rows, k), F32),
            pltpu.VMEM((STREAMS, n_grp - 1, rows, k), F32),
            pltpu.SemaphoreType.DMA((3 + 2 * levels,)),
            pltpu.SemaphoreType.DMA((copies,)),
            pltpu.SemaphoreType.DMA((copies,)),
        ],
        compiler_params=pltpu.CompilerParams(
            collective_id=0, has_side_effects=True, vmem_limit_bytes=60 * 2**20),
        cost_estimate=pl.CostEstimate(flops=30 * 2 * k**3, bytes_accessed=10 * 2**20, transcendentals=0),
    )(matrix, leaf_basis, leaf_tri, inner_basis, inner_tri, outer_basis, outer_tri)
    if not scatter:
        narrow = panel // (n_leaf * n_grp) // STREAMS
        result = result.reshape(STREAMS, rows, k)
        result = lax.dynamic_slice_in_dim(result, lax.axis_index("grp") * narrow, narrow, 1)
        result = result.reshape(STREAMS * narrow, k)
    return result.T


def solution(mesh):
    placed = (
        P(("grp", "leaf"), None),
        P(("grp", "leaf"), None),
        P(("grp", "leaf"), None, None),
        P("grp", "leaf", None, None, None),
        P("grp", "leaf", None, None, None),
        P("grp", "leaf", None, None, None),
        P("grp", "leaf", None, None, None),
    )
    return jax.shard_map(
        per_device, mesh=mesh, in_specs=placed, out_specs=P(None, ("grp", "leaf")), check_vma=False
    )
```

```python
import functools

import jax
import jax.numpy as jnp
from jax import lax
from jax.experimental import pallas as pl
from jax.experimental.pallas import tpu as pltpu
from jax.sharding import PartitionSpec as P

MESH = pl.DeviceIdType.MESH
F32 = jnp.float32
BF16 = jnp.bfloat16
STREAMS = 2


def dot(left, right):
    return jnp.dot(left, right, preferred_element_type=F32)


def dot_nt(left, right):
    return lax.dot_general(left, right, (((1,), (1,)), ((), ())), preferred_element_type=F32)


def twice(values, product, weights):
    count = values.shape[0]
    high = values.astype(BF16).astype(F32)
    both = product(jnp.concatenate([high, values - high], axis=0).astype(BF16), weights)
    return both[:count] + both[count:]


def bit_of(index, height):
    return lax.rem(lax.div(index, 2**height), 2)


def flipped(index, mask):
    for height in range(mask.bit_length()):
        if mask >> height & 1:
            index = index + 2**height * (1 - 2 * bit_of(index, height))
    return index


def reversed_bits(index, count):
    return sum((index >> i & 1) << (count - 1 - i) for i in range(count))


def plan(panel, n_leaf, n_grp):
    inner_rows = panel // n_leaf // STREAMS
    return inner_rows, inner_rows // n_grp >= 8


def axis_orders(bits):
    half = (len(bits) + 1) // 2
    return (bits, bits[half:] + bits[:half])


def kernel(n_leaf, n_grp, *refs):
    (matrix, leaf_basis, leaf_tri, inner_basis, inner_tri, outer_basis, outer_tri, out,
     panel_v, leaf_v, leaf_f, node_v, node_f, outer_high, outer_low, first, kept, first_in, parts, parts_in,
     last, last_in, load_sem, send_sem, recv_sem) = refs
    panel = matrix.shape[1]
    k = leaf_tri.shape[-1]
    inner, outer = n_leaf.bit_length() - 1, n_grp.bit_length() - 1
    inner_rows, scatter = plan(panel, n_leaf, n_grp)
    leaf, grp = lax.axis_index("leaf"), lax.axis_index("grp")

    barrier = pltpu.get_barrier_semaphore()
    for height in range(inner):
        pl.semaphore_signal(barrier, inc=1, device_id={"leaf": flipped(leaf, 1 << height)}, device_id_type=MESH)
    for mask in range(1, n_grp):
        pl.semaphore_signal(barrier, inc=1, device_id={"grp": flipped(grp, mask)}, device_id_type=MESH)

    pairs = [(matrix, panel_v), (leaf_basis, leaf_v), (leaf_tri.at[0], leaf_f)]
    for height in range(inner):
        pairs.append((inner_basis.at[0, 0, height], node_v.at[height]))
        pairs.append((inner_tri.at[0, 0, height], node_f.at[height]))
    for height in range(outer):
        pairs.append((outer_basis.at[0, 0, height], node_v.at[inner + height]))
        pairs.append((outer_tri.at[0, 0, height], node_f.at[inner + height]))
    loads = [pltpu.make_async_copy(src, dst, load_sem.at[i]) for i, (src, dst) in enumerate(pairs)]
    for load in loads[:3]:
        load.start()

    sent = []

    def send(src, dst, device):
        slot = len(sent)
        copy = pltpu.make_async_remote_copy(
            src_ref=src, dst_ref=dst, send_sem=send_sem.at[slot], recv_sem=recv_sem.at[slot],
            device_id=device, device_id_type=MESH)
        copy.start()
        sent.append(copy)
        return copy

    columns = lax.broadcasted_iota(jnp.int32, (1, panel), 1)
    half = panel // 2
    stream_rows = half // STREAMS
    width = panel // (n_leaf * n_grp)
    narrow = width // STREAMS
    owner, place = lax.div(columns, width), lax.rem(columns, width)
    target = lax.div(place, narrow) * stream_rows + lax.rem(place, narrow)
    for height in range(inner + outer):
        bit = bit_of(owner, height)
        if height < inner or scatter:
            mine = bit_of(leaf, height) if height < inner else bit_of(grp, height - inner)
            target = target + (bit + mine - 2 * bit * mine) * (stream_rows >> height if height else half)
        else:
            target = target + bit * (narrow << (height - inner))
    streams = range(STREAMS)

    def load_node(level):
        loads[3 + 2 * level].wait()
        loads[4 + 2 * level].wait()

    def half_basis(level, parity):
        return node_v[level, pl.ds(pl.multiple_of(parity * k, k), k), :]

    rows = lax.broadcasted_iota(jnp.int32, (panel, panel), 0)
    order = jnp.where(rows == target, 1.0, 0.0).astype(BF16)
    loads[0].wait()
    turned = dot_nt(order, panel_v[...]).astype(BF16)
    loads[1].wait()
    loads[2].wait()
    for load in loads[3:]:
        load.start()
    projected = dot(turned, leaf_v[...])

    def leaf_summit(span):
        mixing = twice(projected[span], dot, leaf_f[...])
        return turned[span, :k].astype(F32) - twice(mixing, dot_nt, leaf_v[:k, :])

    first[...] = leaf_summit(slice(half, panel))
    pl.semaphore_wait(barrier, inner + n_grp - 1)
    arriving = send(first, first_in, {"leaf": flipped(leaf, 1)})
    kept[...] = leaf_summit(slice(0, half))

    def own_mixing(summit, level, parity):
        projected = twice(summit, dot, half_basis(level, parity))
        return twice(projected, dot, node_f[level]), jnp.where(parity == 0, summit, 0.0)

    bits = tuple(range(1, inner))
    orders = axis_orders(bits)
    lanes = k // 2
    left = [[list(bits) for _ in orders] for _ in streams]
    waiting = [[None, None] for _ in streams]

    def pick(stream, group, height, side):
        return (slice(None),) * left[stream][group].index(height) + (side,)

    def send_part(stream, group, step):
        height = orders[group][step]
        waiting[stream][group] = send(
            parts[stream][group][step].at[pick(stream, group, height, 1)], parts_in[stream][group][step],
            {"leaf": flipped(leaf, 1 << height)})

    for level in range(inner):
        load_node(level)
    parity = bit_of(leaf, 0)
    projected = twice(kept[...], dot, half_basis(0, parity))
    arriving.wait_recv()
    projected = projected + twice(first_in[...], dot, half_basis(0, 1 - parity))
    mixing = twice(projected, dot, node_f[0])
    top = jnp.where(parity == 0, kept[...], first_in[...])
    summit = top - twice(mixing, dot_nt, node_v[0, :k, :])
    for level in range(1, inner - 1):
        mixing, top = own_mixing(summit, level, bit_of(leaf, level))
        summit = top - twice(mixing, dot_nt, node_v[level, :k, :])
    level = inner - 1
    mixing, top = own_mixing(summit, level, bit_of(leaf, level))
    for group in range(2):
        span = slice(group * lanes, (group + 1) * lanes)
        term = top[:, span] - twice(mixing, dot_nt, node_v[level, span, :])
        for stream in streams:
            part = term[stream * stream_rows:(stream + 1) * stream_rows]
            parts[stream][group][0][...] = part.reshape(parts[stream][group][0].shape)
            send_part(stream, group, 0)

    def outer_term(height):
        level, parity = inner + height, bit_of(grp, height)
        load_node(level)
        rows = lax.broadcasted_iota(jnp.int32, (k, k), 0)
        lane = lax.broadcasted_iota(jnp.int32, (k, k), 1)
        joint = dot_nt(node_f[level], node_v[level, :k, :])
        high = joint.astype(BF16)
        low = (joint - high.astype(F32)).astype(BF16)
        basis = half_basis(level, parity)
        matrix = jnp.where((rows == lane) & (parity == 0), 1.0, 0.0) - (dot(basis, high) + dot(basis, low))
        high = matrix.astype(BF16)
        outer_high[height] = high
        outer_low[height] = (matrix - high.astype(F32)).astype(BF16)

    def apply_outer(summit, height):
        return twice(summit, dot, outer_high[height]) + dot(summit.astype(BF16), outer_low[height])

    sums = [[None, None] for _ in streams]
    coming = [[] for _ in streams]
    ahead = list(range(outer))
    for step in range(len(bits)):
        for stream in streams:
            if ahead:
                outer_term(ahead.pop(0))
            for group in range(2):
                height = orders[group][step]
                waiting[stream][group].wait_recv()
                total = parts[stream][group][step][pick(stream, group, height, 0)] + parts_in[stream][group][step][...]
                left[stream][group].remove(height)
                if step + 1 < len(bits):
                    parts[stream][group][step + 1][...] = total
                    send_part(stream, group, step + 1)
                else:
                    sums[stream][group] = total
            if step + 1 == len(bits):
                summit = jnp.concatenate(sums[stream], axis=1)
                for height in range(outer):
                    summit = apply_outer(summit, height)
                last[stream] = summit.reshape(last.shape[1:])
                for mask in range(1, n_grp):
                    piece = reversed_bits(mask, outer) if scatter else 0
                    coming[stream].append(send(
                        last.at[stream, piece], last_in.at[stream, mask - 1], {"grp": flipped(grp, mask)}))
    totals = []
    for stream in streams:
        total = last[stream, 0]
        for slot, copy in enumerate(coming[stream]):
            copy.wait_recv()
            total = total + last_in[stream, slot]
        totals.append(total)
    out[...] = jnp.concatenate(totals, axis=0).astype(out.dtype)
    for copy in sent:
        copy.wait_send()


def per_device(matrix, leaf_basis, leaf_tri, inner_basis, inner_tri, outer_basis, outer_tri):
    n_leaf, n_grp = lax.axis_size("leaf"), lax.axis_size("grp")
    panel, k = matrix.shape[1], leaf_tri.shape[-1]
    inner, outer = n_leaf.bit_length() - 1, n_grp.bit_length() - 1
    inner_rows, scatter = plan(panel, n_leaf, n_grp)
    levels = inner + outer
    rows = inner_rows // n_grp if scatter else inner_rows
    half = panel // 2
    lead = lambda count: (2,) * count + (inner_rows, k // 2)
    steps = range(inner - 1)
    parts = [[[pltpu.VMEM(lead(inner - 1 - s), F32) for s in steps] for _ in range(2)] for _ in range(STREAMS)]
    parts_in = [[[pltpu.VMEM(lead(inner - 2 - s), F32) for s in steps] for _ in range(2)] for _ in range(STREAMS)]
    copies = 1 + STREAMS * (2 * (inner - 1) + n_grp - 1)
    result = pl.pallas_call(
        functools.partial(kernel, n_leaf, n_grp),
        out_shape=jax.ShapeDtypeStruct((STREAMS * rows, k), BF16),
        in_specs=[pl.BlockSpec(memory_space=pl.ANY)] * 7,
        out_specs=pl.BlockSpec(memory_space=pltpu.VMEM),
        scratch_shapes=[
            pltpu.VMEM(matrix.shape, BF16),
            pltpu.VMEM(leaf_basis.shape, BF16),
            pltpu.VMEM(leaf_tri.shape[1:], BF16),
            pltpu.VMEM((levels,) + inner_basis.shape[-2:], BF16),
            pltpu.VMEM((levels,) + inner_tri.shape[-2:], BF16),
            pltpu.VMEM((outer, k, k), BF16),
            pltpu.VMEM((outer, k, k), BF16),
            pltpu.VMEM((half, k), F32),
            pltpu.VMEM((half, k), F32),
            pltpu.VMEM((half, k), F32),
            parts,
            parts_in,
            pltpu.VMEM((STREAMS, n_grp if scatter else 1, rows, k), F32),
            pltpu.VMEM((STREAMS, n_grp - 1, rows, k), F32),
            pltpu.SemaphoreType.DMA((3 + 2 * levels,)),
            pltpu.SemaphoreType.DMA((copies,)),
            pltpu.SemaphoreType.DMA((copies,)),
        ],
        compiler_params=pltpu.CompilerParams(
            collective_id=0, has_side_effects=True, vmem_limit_bytes=60 * 2**20),
        cost_estimate=pl.CostEstimate(flops=30 * 2 * k**3, bytes_accessed=10 * 2**20, transcendentals=0),
    )(matrix, leaf_basis, leaf_tri, inner_basis, inner_tri, outer_basis, outer_tri)
    if not scatter:
        narrow = panel // (n_leaf * n_grp) // STREAMS
        result = result.reshape(STREAMS, rows, k)
        result = lax.dynamic_slice_in_dim(result, lax.axis_index("grp") * narrow, narrow, 1)
        result = result.reshape(STREAMS * narrow, k)
    return result.T


def solution(mesh):
    placed = (
        P(("grp", "leaf"), None),
        P(("grp", "leaf"), None),
        P(("grp", "leaf"), None, None),
        P("grp", "leaf", None, None, None),
        P("grp", "leaf", None, None, None),
        P("grp", "leaf", None, None, None),
        P("grp", "leaf", None, None, None),
    )
    return jax.shard_map(
        per_device, mesh=mesh, in_specs=placed, out_specs=P(None, ("grp", "leaf")), check_vma=False
    )
```

```python
import functools

import jax
import jax.numpy as jnp
from jax import lax
from jax.experimental import pallas as pl
from jax.experimental.pallas import tpu as pltpu
from jax.sharding import PartitionSpec as P

MESH = pl.DeviceIdType.MESH
F32 = jnp.float32
BF16 = jnp.bfloat16
STREAMS = 2


def dot(left, right):
    return jnp.dot(left, right, preferred_element_type=F32)


def dot_nt(left, right):
    return lax.dot_general(left, right, (((1,), (1,)), ((), ())), preferred_element_type=F32)


def dot_upper(left, right):
    mid = right.shape[0] // 2
    return jnp.concatenate([dot(left[:, :mid], right[:mid, :mid]), dot(left, right[:, mid:])], axis=1)


def twice(values, product, weights):
    count = values.shape[0]
    high = values.astype(BF16)
    low = values - high.astype(F32)
    if count % 16:
        stacked = jnp.concatenate([high.astype(F32), low], axis=0).astype(BF16)
    else:
        stacked = jnp.concatenate([high, low.astype(BF16)], axis=0)
    both = product(stacked, weights)
    return both[:count] + both[count:]


def bit_of(index, height):
    return lax.rem(lax.div(index, 2**height), 2)


def flipped(index, mask):
    for height in range(mask.bit_length()):
        if mask >> height & 1:
            index = index + 2**height * (1 - 2 * bit_of(index, height))
    return index


def reversed_bits(index, count):
    return sum((index >> i & 1) << (count - 1 - i) for i in range(count))


def plan(panel, n_leaf, n_grp):
    inner_rows = panel // n_leaf // STREAMS
    return inner_rows, inner_rows // n_grp >= 8


def axis_orders(bits):
    half = (len(bits) + 1) // 2
    return (bits, bits[half:] + bits[:half])


def kernel(n_leaf, n_grp, *refs):
    (matrix, leaf_basis, leaf_tri, inner_basis, inner_tri, outer_basis, outer_tri, out,
     panel_v, leaf_v, leaf_f, node_v, node_f, outer_high, outer_low, first, kept, first_in, parts, parts_in,
     last, last_in, load_sem, send_sem, recv_sem) = refs
    panel = matrix.shape[1]
    k = leaf_tri.shape[-1]
    inner, outer = n_leaf.bit_length() - 1, n_grp.bit_length() - 1
    inner_rows, scatter = plan(panel, n_leaf, n_grp)
    leaf, grp = lax.axis_index("leaf"), lax.axis_index("grp")

    barrier = pltpu.get_barrier_semaphore()
    for height in range(inner):
        pl.semaphore_signal(barrier, inc=1, device_id={"leaf": flipped(leaf, 1 << height)}, device_id_type=MESH)
    for mask in range(1, n_grp):
        pl.semaphore_signal(barrier, inc=1, device_id={"grp": flipped(grp, mask)}, device_id_type=MESH)

    pairs = [(matrix, panel_v), (leaf_basis, leaf_v), (leaf_tri.at[0], leaf_f)]
    for height in range(inner):
        pairs.append((inner_basis.at[0, 0, height], node_v.at[height]))
        pairs.append((inner_tri.at[0, 0, height], node_f.at[height]))
    for height in range(outer):
        pairs.append((outer_basis.at[0, 0, height], node_v.at[inner + height]))
        pairs.append((outer_tri.at[0, 0, height], node_f.at[inner + height]))
    loads = [pltpu.make_async_copy(src, dst, load_sem.at[i]) for i, (src, dst) in enumerate(pairs)]
    for load in loads[:3]:
        load.start()

    sent = []

    def send(src, dst, device):
        slot = len(sent)
        copy = pltpu.make_async_remote_copy(
            src_ref=src, dst_ref=dst, send_sem=send_sem.at[slot], recv_sem=recv_sem.at[slot],
            device_id=device, device_id_type=MESH)
        copy.start()
        sent.append(copy)
        return copy

    columns = lax.broadcasted_iota(jnp.int32, (1, panel), 1)
    half = panel // 2
    stream_rows = half // STREAMS
    width = panel // (n_leaf * n_grp)
    narrow = width // STREAMS
    owner, place = lax.div(columns, width), lax.rem(columns, width)
    target = lax.div(place, narrow) * stream_rows + lax.rem(place, narrow)
    for height in range(inner + outer):
        bit = bit_of(owner, height)
        if height < inner or scatter:
            mine = bit_of(leaf, height) if height < inner else bit_of(grp, height - inner)
            target = target + (bit + mine - 2 * bit * mine) * (stream_rows >> height if height else half)
        else:
            target = target + bit * (narrow << (height - inner))
    streams = range(STREAMS)

    def load_node(level):
        loads[3 + 2 * level].wait()
        loads[4 + 2 * level].wait()

    def half_basis(level, parity):
        return node_v[level, pl.ds(pl.multiple_of(parity * k, k), k), :]

    rows = lax.broadcasted_iota(jnp.int32, (panel, panel), 0)
    order = jnp.where(rows == target, 1.0, 0.0).astype(BF16)
    loads[0].wait()
    turned = dot_nt(order, panel_v[...]).astype(BF16)
    loads[1].wait()
    loads[2].wait()
    for load in loads[3:]:
        load.start()
    projected = dot(turned, leaf_v[...])

    def leaf_summit(span):
        mixing = twice(projected[span], dot_upper, leaf_f)
        return turned[span, :k].astype(F32) - twice(mixing, dot_nt, leaf_v[:k, :])

    first[...] = leaf_summit(slice(half, panel))
    pl.semaphore_wait(barrier, inner + n_grp - 1)
    arriving = send(first, first_in, {"leaf": flipped(leaf, 1)})
    kept[...] = leaf_summit(slice(0, half))

    def own_mixing(summit, level, parity):
        projected = twice(summit, dot, half_basis(level, parity))
        return twice(projected, dot_upper, node_f.at[level]), jnp.where(parity == 0, summit, 0.0)

    bits = tuple(range(1, inner))
    orders = axis_orders(bits)
    lanes = k // 2
    left = [[list(bits) for _ in orders] for _ in streams]
    waiting = [[None, None] for _ in streams]

    def pick(stream, group, height, side):
        return (slice(None),) * left[stream][group].index(height) + (side,)

    def send_part(stream, group, step):
        height = orders[group][step]
        waiting[stream][group] = send(
            parts[stream][group][step].at[pick(stream, group, height, 1)], parts_in[stream][group][step],
            {"leaf": flipped(leaf, 1 << height)})

    for level in range(inner):
        load_node(level)
    parity = bit_of(leaf, 0)
    projected = twice(kept[...], dot, half_basis(0, parity))
    arriving.wait_recv()
    projected = projected + twice(first_in[...], dot, half_basis(0, 1 - parity))
    mixing = twice(projected, dot_upper, node_f.at[0])
    top = jnp.where(parity == 0, kept[...], first_in[...])
    summit = top - twice(mixing, dot_nt, node_v[0, :k, :])
    for stream in streams:
        term = summit[stream * stream_rows:(stream + 1) * stream_rows]
        for level in range(1, inner - 1):
            mixing, top = own_mixing(term, level, bit_of(leaf, level))
            term = top - twice(mixing, dot_nt, node_v[level, :k, :])
        level = inner - 1
        mixing, top = own_mixing(term, level, bit_of(leaf, level))
        for group in range(2):
            span = slice(group * lanes, (group + 1) * lanes)
            part = top[:, span] - twice(mixing, dot_nt, node_v[level, span, :])
            parts[stream][group][0][...] = part.reshape(parts[stream][group][0].shape)
            send_part(stream, group, 0)

    def outer_term(height):
        level, parity = inner + height, bit_of(grp, height)
        load_node(level)
        rows = lax.broadcasted_iota(jnp.int32, (k, k), 0)
        lane = lax.broadcasted_iota(jnp.int32, (k, k), 1)
        mid = k // 2
        joint = jnp.concatenate([
            dot_nt(node_f[level, :mid, :], node_v[level, :k, :]),
            dot_nt(node_f[level, mid:, mid:], node_v[level, :k, mid:])], axis=0)
        high = joint.astype(BF16)
        low = (joint - high.astype(F32)).astype(BF16)
        basis = half_basis(level, parity)
        matrix = jnp.where((rows == lane) & (parity == 0), 1.0, 0.0) - (dot(basis, high) + dot(basis, low))
        high = matrix.astype(BF16)
        outer_high[height] = high
        outer_low[height] = (matrix - high.astype(F32)).astype(BF16)

    def apply_outer(summit, height):
        return twice(summit, dot, outer_high[height]) + dot(summit.astype(BF16), outer_low[height])

    sums = [[None, None] for _ in streams]
    coming = [[] for _ in streams]
    ahead = list(range(outer))
    for step in range(len(bits)):
        for stream in streams:
            for group in range(2):
                height = orders[group][step]
                waiting[stream][group].wait_recv()
                total = parts[stream][group][step][pick(stream, group, height, 0)] + parts_in[stream][group][step][...]
                left[stream][group].remove(height)
                if step + 1 < len(bits):
                    parts[stream][group][step + 1][...] = total
                    send_part(stream, group, step + 1)
                else:
                    sums[stream][group] = total
            if ahead:
                outer_term(ahead.pop(0))
            if step + 1 == len(bits):
                summit = jnp.concatenate(sums[stream], axis=1)
                for height in range(outer):
                    summit = apply_outer(summit, height)
                last[stream] = summit.reshape(last.shape[1:])
                for mask in range(1, n_grp):
                    piece = reversed_bits(mask, outer) if scatter else 0
                    coming[stream].append(send(
                        last.at[stream, piece], last_in.at[stream, mask - 1], {"grp": flipped(grp, mask)}))
    totals = []
    for stream in streams:
        total = last[stream, 0]
        for slot, copy in enumerate(coming[stream]):
            copy.wait_recv()
            total = total + last_in[stream, slot]
        totals.append(total)
    out[...] = jnp.concatenate(totals, axis=0).astype(out.dtype)
    for copy in sent:
        copy.wait_send()


def per_device(matrix, leaf_basis, leaf_tri, inner_basis, inner_tri, outer_basis, outer_tri):
    n_leaf, n_grp = lax.axis_size("leaf"), lax.axis_size("grp")
    panel, k = matrix.shape[1], leaf_tri.shape[-1]
    inner, outer = n_leaf.bit_length() - 1, n_grp.bit_length() - 1
    inner_rows, scatter = plan(panel, n_leaf, n_grp)
    levels = inner + outer
    rows = inner_rows // n_grp if scatter else inner_rows
    half = panel // 2
    lead = lambda count: (2,) * count + (inner_rows, k // 2)
    steps = range(inner - 1)
    parts = [[[pltpu.VMEM(lead(inner - 1 - s), F32) for s in steps] for _ in range(2)] for _ in range(STREAMS)]
    parts_in = [[[pltpu.VMEM(lead(inner - 2 - s), F32) for s in steps] for _ in range(2)] for _ in range(STREAMS)]
    copies = 1 + STREAMS * (2 * (inner - 1) + n_grp - 1)
    result = pl.pallas_call(
        functools.partial(kernel, n_leaf, n_grp),
        out_shape=jax.ShapeDtypeStruct((STREAMS * rows, k), BF16),
        in_specs=[pl.BlockSpec(memory_space=pl.ANY)] * 7,
        out_specs=pl.BlockSpec(memory_space=pltpu.VMEM),
        scratch_shapes=[
            pltpu.VMEM(matrix.shape, BF16),
            pltpu.VMEM(leaf_basis.shape, BF16),
            pltpu.VMEM(leaf_tri.shape[1:], BF16),
            pltpu.VMEM((levels,) + inner_basis.shape[-2:], BF16),
            pltpu.VMEM((levels,) + inner_tri.shape[-2:], BF16),
            pltpu.VMEM((outer, k, k), BF16),
            pltpu.VMEM((outer, k, k), BF16),
            pltpu.VMEM((half, k), F32),
            pltpu.VMEM((half, k), F32),
            pltpu.VMEM((half, k), F32),
            parts,
            parts_in,
            pltpu.VMEM((STREAMS, n_grp if scatter else 1, rows, k), F32),
            pltpu.VMEM((STREAMS, n_grp - 1, rows, k), F32),
            pltpu.SemaphoreType.DMA((3 + 2 * levels,)),
            pltpu.SemaphoreType.DMA((copies,)),
            pltpu.SemaphoreType.DMA((copies,)),
        ],
        compiler_params=pltpu.CompilerParams(
            collective_id=0, has_side_effects=True, vmem_limit_bytes=60 * 2**20),
        cost_estimate=pl.CostEstimate(flops=30 * 2 * k**3, bytes_accessed=10 * 2**20, transcendentals=0),
    )(matrix, leaf_basis, leaf_tri, inner_basis, inner_tri, outer_basis, outer_tri)
    if not scatter:
        narrow = panel // (n_leaf * n_grp) // STREAMS
        result = result.reshape(STREAMS, rows, k)
        result = lax.dynamic_slice_in_dim(result, lax.axis_index("grp") * narrow, narrow, 1)
        result = result.reshape(STREAMS * narrow, k)
    return result.T


def solution(mesh):
    placed = (
        P(("grp", "leaf"), None),
        P(("grp", "leaf"), None),
        P(("grp", "leaf"), None, None),
        P("grp", "leaf", None, None, None),
        P("grp", "leaf", None, None, None),
        P("grp", "leaf", None, None, None),
        P("grp", "leaf", None, None, None),
    )
    return jax.shard_map(
        per_device, mesh=mesh, in_specs=placed, out_specs=P(None, ("grp", "leaf")), check_vma=False
    )
```

```python
import functools

import jax
import jax.numpy as jnp
from jax import lax
from jax.experimental import pallas as pl
from jax.experimental.pallas import tpu as pltpu
from jax.sharding import PartitionSpec as P

MESH = pl.DeviceIdType.MESH
F32 = jnp.float32
BF16 = jnp.bfloat16
STREAMS = 2


def dot(left, right):
    return jnp.dot(left, right, preferred_element_type=F32)


def dot_nt(left, right):
    return lax.dot_general(left, right, (((1,), (1,)), ((), ())), preferred_element_type=F32)


def stack(values):
    high = values.astype(BF16)
    low = values - high.astype(F32)
    if values.shape[0] % 16:
        return jnp.concatenate([high.astype(F32), low], axis=0).astype(BF16)
    return jnp.concatenate([high, low.astype(BF16)], axis=0)


def fold(both):
    count = both.shape[0] // 2
    return both[:count] + both[count:]


def join(tiles):
    return jnp.concatenate(tiles, axis=1)


def mix(projected, factor):
    mid = factor.shape[0] // 2
    low_tile, high_tile = [stack(tile) for tile in projected]
    first = stack(fold(dot(low_tile, factor[:mid, :mid])))
    return join([first, stack(fold(dot(join([low_tile, high_tile]), factor[:, mid:])))])


def bit_of(index, height):
    return lax.rem(lax.div(index, 2**height), 2)


def flipped(index, mask):
    for height in range(mask.bit_length()):
        if mask >> height & 1:
            index = index + 2**height * (1 - 2 * bit_of(index, height))
    return index


def reversed_bits(index, count):
    return sum((index >> i & 1) << (count - 1 - i) for i in range(count))


def plan(panel, n_leaf, n_grp):
    inner_rows = panel // n_leaf // STREAMS
    return inner_rows, inner_rows // n_grp >= 8


def axis_orders(bits):
    half = (len(bits) + 1) // 2
    return (bits, bits[half:] + bits[:half])


def kernel(n_leaf, n_grp, *refs):
    (matrix, leaf_basis, leaf_tri, inner_basis, inner_tri, outer_basis, outer_tri, out,
     panel_v, leaf_v, leaf_f, node_v, node_f, outer_high, outer_low, first, kept, first_in, parts, parts_in,
     last, last_in, load_sem, send_sem, recv_sem) = refs
    panel = matrix.shape[1]
    k = leaf_tri.shape[-1]
    inner, outer = n_leaf.bit_length() - 1, n_grp.bit_length() - 1
    inner_rows, scatter = plan(panel, n_leaf, n_grp)
    leaf, grp = lax.axis_index("leaf"), lax.axis_index("grp")

    barrier = pltpu.get_barrier_semaphore()
    for height in range(inner):
        pl.semaphore_signal(barrier, inc=1, device_id={"leaf": flipped(leaf, 1 << height)}, device_id_type=MESH)
    for mask in range(1, n_grp):
        pl.semaphore_signal(barrier, inc=1, device_id={"grp": flipped(grp, mask)}, device_id_type=MESH)

    pairs = [(matrix, panel_v), (leaf_basis, leaf_v), (leaf_tri.at[0], leaf_f)]
    for height in range(inner):
        pairs.append((inner_basis.at[0, 0, height], node_v.at[height]))
        pairs.append((inner_tri.at[0, 0, height], node_f.at[height]))
    for height in range(outer):
        pairs.append((outer_basis.at[0, 0, height], node_v.at[inner + height]))
        pairs.append((outer_tri.at[0, 0, height], node_f.at[inner + height]))
    loads = [pltpu.make_async_copy(src, dst, load_sem.at[i]) for i, (src, dst) in enumerate(pairs)]
    for load in loads[:3]:
        load.start()

    sent = []

    def send(src, dst, device):
        slot = len(sent)
        copy = pltpu.make_async_remote_copy(
            src_ref=src, dst_ref=dst, send_sem=send_sem.at[slot], recv_sem=recv_sem.at[slot],
            device_id=device, device_id_type=MESH)
        copy.start()
        sent.append(copy)
        return copy

    columns = lax.broadcasted_iota(jnp.int32, (1, panel), 1)
    half = panel // 2
    stream_rows = half // STREAMS
    width = panel // (n_leaf * n_grp)
    narrow = width // STREAMS
    owner, place = lax.div(columns, width), lax.rem(columns, width)
    target = lax.div(place, narrow) * stream_rows + lax.rem(place, narrow)
    for height in range(inner + outer):
        bit = bit_of(owner, height)
        if height < inner or scatter:
            mine = bit_of(leaf, height) if height < inner else bit_of(grp, height - inner)
            target = target + (bit + mine - 2 * bit * mine) * (stream_rows >> height if height else half)
        else:
            target = target + bit * (narrow << (height - inner))
    streams = range(STREAMS)

    def load_node(level):
        loads[3 + 2 * level].wait()
        loads[4 + 2 * level].wait()

    def half_basis(level, parity, span=slice(None)):
        return node_v[level, pl.ds(pl.multiple_of(parity * k, k), k), span]

    rows = lax.broadcasted_iota(jnp.int32, (panel, panel), 0)
    order = jnp.where(rows == target, 1.0, 0.0).astype(BF16)
    loads[0].wait()
    turned = dot_nt(order, panel_v[...]).astype(BF16)
    loads[1].wait()
    loads[2].wait()
    for load in loads[3:]:
        load.start()
    projected = dot(turned, leaf_v[...])

    mid = k // 2
    spans = (slice(0, mid), slice(mid, k))

    def leaf_summit(ref, rows):
        mixing = mix([projected[rows, span] for span in spans], leaf_f)
        for span in spans:
            ref[:, span] = turned[rows, span].astype(F32) - fold(dot_nt(mixing, leaf_v[span, :]))

    leaf_summit(first, slice(half, panel))
    pl.semaphore_wait(barrier, inner + n_grp - 1)
    arriving = send(first, first_in, {"leaf": flipped(leaf, 1)})
    leaf_summit(kept, slice(0, half))

    def project(stacked, level, parity):
        return [fold(dot(stacked, half_basis(level, parity, span))) for span in spans]

    def own_term(tiles, level):
        parity = bit_of(leaf, level)
        mixing = mix(project(join([stack(tile) for tile in tiles]), level, parity), node_f.at[level])
        for tile, span in zip(tiles, spans):
            yield jnp.where(parity == 0, tile, 0.0) - fold(dot_nt(mixing, node_v[level, span, :]))

    bits = tuple(range(1, inner))
    orders = axis_orders(bits)
    left = [[list(bits) for _ in orders] for _ in streams]
    waiting = [[None, None] for _ in streams]

    def pick(stream, group, height, side):
        return (slice(None),) * left[stream][group].index(height) + (side,)

    def send_part(stream, group, step):
        height = orders[group][step]
        waiting[stream][group] = send(
            parts[stream][group][step].at[pick(stream, group, height, 1)], parts_in[stream][group][step],
            {"leaf": flipped(leaf, 1 << height)})

    for level in range(inner):
        load_node(level)
    parity = bit_of(leaf, 0)
    own = project(stack(kept[...]), 0, parity)
    arriving.wait_recv()
    other = project(stack(first_in[...]), 0, 1 - parity)
    mixing = mix([left_tile + right_tile for left_tile, right_tile in zip(own, other)], node_f.at[0])
    summit = [
        jnp.where(parity == 0, kept[:, span], first_in[:, span]) - fold(dot_nt(mixing, node_v[0, span, :]))
        for span in spans]
    for stream in streams:
        tiles = [tile[stream * stream_rows:(stream + 1) * stream_rows] for tile in summit]
        for level in range(1, inner - 1):
            tiles = list(own_term(tiles, level))
        for group, tile in enumerate(own_term(tiles, inner - 1)):
            parts[stream][group][0][...] = tile.reshape(parts[stream][group][0].shape)
            send_part(stream, group, 0)

    def outer_term(height):
        level, parity = inner + height, bit_of(grp, height)
        load_node(level)
        rows = lax.broadcasted_iota(jnp.int32, (k, k), 0)
        lane = lax.broadcasted_iota(jnp.int32, (k, k), 1)
        joint = jnp.concatenate([
            dot_nt(node_f[level, :mid, :], node_v[level, :k, :]),
            dot_nt(node_f[level, mid:, mid:], node_v[level, :k, mid:])], axis=0)
        high = joint.astype(BF16)
        low = (joint - high.astype(F32)).astype(BF16)
        basis = half_basis(level, parity)
        matrix = jnp.where((rows == lane) & (parity == 0), 1.0, 0.0) - (dot(basis, high) + dot(basis, low))
        high = matrix.astype(BF16)
        outer_high[height] = high
        outer_low[height] = (matrix - high.astype(F32)).astype(BF16)

    def apply_outer(summit, height):
        stacked = stack(summit)
        return fold(dot(stacked, outer_high[height])) + dot(stacked[:summit.shape[0]], outer_low[height])

    sums = [[None, None] for _ in streams]
    coming = [[] for _ in streams]
    ahead = list(range(outer))
    for step in range(len(bits)):
        for stream in streams:
            for group in range(2):
                height = orders[group][step]
                waiting[stream][group].wait_recv()
                total = parts[stream][group][step][pick(stream, group, height, 0)] + parts_in[stream][group][step][...]
                left[stream][group].remove(height)
                if step + 1 < len(bits):
                    parts[stream][group][step + 1][...] = total
                    send_part(stream, group, step + 1)
                else:
                    sums[stream][group] = total
            if ahead:
                outer_term(ahead.pop(0))
            if step + 1 == len(bits):
                summit = jnp.concatenate(sums[stream], axis=1)
                for height in range(outer):
                    summit = apply_outer(summit, height)
                last[stream] = summit.reshape(last.shape[1:])
                for mask in range(1, n_grp):
                    piece = reversed_bits(mask, outer) if scatter else 0
                    coming[stream].append(send(
                        last.at[stream, piece], last_in.at[stream, mask - 1], {"grp": flipped(grp, mask)}))
    totals = []
    for stream in streams:
        total = last[stream, 0]
        for slot, copy in enumerate(coming[stream]):
            copy.wait_recv()
            total = total + last_in[stream, slot]
        totals.append(total)
    out[...] = jnp.concatenate(totals, axis=0).astype(out.dtype)
    for copy in sent:
        copy.wait_send()


def per_device(matrix, leaf_basis, leaf_tri, inner_basis, inner_tri, outer_basis, outer_tri):
    n_leaf, n_grp = lax.axis_size("leaf"), lax.axis_size("grp")
    panel, k = matrix.shape[1], leaf_tri.shape[-1]
    inner, outer = n_leaf.bit_length() - 1, n_grp.bit_length() - 1
    inner_rows, scatter = plan(panel, n_leaf, n_grp)
    levels = inner + outer
    rows = inner_rows // n_grp if scatter else inner_rows
    half = panel // 2
    lead = lambda count: (2,) * count + (inner_rows, k // 2)
    steps = range(inner - 1)
    parts = [[[pltpu.VMEM(lead(inner - 1 - s), F32) for s in steps] for _ in range(2)] for _ in range(STREAMS)]
    parts_in = [[[pltpu.VMEM(lead(inner - 2 - s), F32) for s in steps] for _ in range(2)] for _ in range(STREAMS)]
    copies = 1 + STREAMS * (2 * (inner - 1) + n_grp - 1)
    result = pl.pallas_call(
        functools.partial(kernel, n_leaf, n_grp),
        out_shape=jax.ShapeDtypeStruct((STREAMS * rows, k), BF16),
        in_specs=[pl.BlockSpec(memory_space=pl.ANY)] * 7,
        out_specs=pl.BlockSpec(memory_space=pltpu.VMEM),
        scratch_shapes=[
            pltpu.VMEM(matrix.shape, BF16),
            pltpu.VMEM(leaf_basis.shape, BF16),
            pltpu.VMEM(leaf_tri.shape[1:], BF16),
            pltpu.VMEM((levels,) + inner_basis.shape[-2:], BF16),
            pltpu.VMEM((levels,) + inner_tri.shape[-2:], BF16),
            pltpu.VMEM((outer, k, k), BF16),
            pltpu.VMEM((outer, k, k), BF16),
            pltpu.VMEM((half, k), F32),
            pltpu.VMEM((half, k), F32),
            pltpu.VMEM((half, k), F32),
            parts,
            parts_in,
            pltpu.VMEM((STREAMS, n_grp if scatter else 1, rows, k), F32),
            pltpu.VMEM((STREAMS, n_grp - 1, rows, k), F32),
            pltpu.SemaphoreType.DMA((3 + 2 * levels,)),
            pltpu.SemaphoreType.DMA((copies,)),
            pltpu.SemaphoreType.DMA((copies,)),
        ],
        compiler_params=pltpu.CompilerParams(
            collective_id=0, has_side_effects=True, vmem_limit_bytes=60 * 2**20),
        cost_estimate=pl.CostEstimate(flops=30 * 2 * k**3, bytes_accessed=10 * 2**20, transcendentals=0),
    )(matrix, leaf_basis, leaf_tri, inner_basis, inner_tri, outer_basis, outer_tri)
    if not scatter:
        narrow = panel // (n_leaf * n_grp) // STREAMS
        result = result.reshape(STREAMS, rows, k)
        result = lax.dynamic_slice_in_dim(result, lax.axis_index("grp") * narrow, narrow, 1)
        result = result.reshape(STREAMS * narrow, k)
    return result.T


def solution(mesh):
    placed = (
        P(("grp", "leaf"), None),
        P(("grp", "leaf"), None),
        P(("grp", "leaf"), None, None),
        P("grp", "leaf", None, None, None),
        P("grp", "leaf", None, None, None),
        P("grp", "leaf", None, None, None),
        P("grp", "leaf", None, None, None),
    )
    return jax.shard_map(
        per_device, mesh=mesh, in_specs=placed, out_specs=P(None, ("grp", "leaf")), check_vma=False
    )
```

```python
import functools

import jax
import jax.numpy as jnp
from jax import lax
from jax.experimental import pallas as pl
from jax.experimental.pallas import tpu as pltpu
from jax.sharding import PartitionSpec as P

MESH = pl.DeviceIdType.MESH
F32 = jnp.float32
BF16 = jnp.bfloat16
STREAMS = 2


def dot(left, right):
    return jnp.dot(left, right, preferred_element_type=F32)


def dot_nt(left, right):
    return lax.dot_general(left, right, (((1,), (1,)), ((), ())), preferred_element_type=F32)


def stack(values):
    high = values.astype(BF16)
    low = values - high.astype(F32)
    if values.shape[0] % 16:
        return jnp.concatenate([high.astype(F32), low], axis=0).astype(BF16)
    return jnp.concatenate([high, low.astype(BF16)], axis=0)


def fold(both):
    count = both.shape[0] // 2
    return both[:count] + both[count:]


def join(tiles):
    return jnp.concatenate(tiles, axis=1)


def mix(projected, factor):
    mid = factor.shape[0] // 2
    low_tile, high_tile = [stack(tile) for tile in projected]
    first = stack(fold(dot(low_tile, factor[:mid, :mid])))
    return join([first, stack(fold(dot(join([low_tile, high_tile]), factor[:, mid:])))])


def bit_of(index, height):
    return lax.rem(lax.div(index, 2**height), 2)


def flipped(index, mask):
    for height in range(mask.bit_length()):
        if mask >> height & 1:
            index = index + 2**height * (1 - 2 * bit_of(index, height))
    return index


def reversed_bits(index, count):
    return sum((index >> i & 1) << (count - 1 - i) for i in range(count))


def plan(panel, n_leaf, n_grp):
    inner_rows = panel // n_leaf // STREAMS
    return inner_rows, inner_rows // n_grp >= 8


def axis_orders(bits):
    half = (len(bits) + 1) // 2
    return (bits, bits[half:] + bits[:half])


def kernel(n_leaf, n_grp, *refs):
    (matrix, leaf_basis, leaf_tri, inner_basis, inner_tri, outer_basis, outer_tri, out,
     panel_v, leaf_v, leaf_f, node_v, node_f, outer_high, outer_low, first, kept, first_in, parts, parts_in,
     last, last_in, load_sem, send_sem, recv_sem) = refs
    panel = matrix.shape[1]
    k = leaf_tri.shape[-1]
    inner, outer = n_leaf.bit_length() - 1, n_grp.bit_length() - 1
    inner_rows, scatter = plan(panel, n_leaf, n_grp)
    leaf, grp = lax.axis_index("leaf"), lax.axis_index("grp")

    barrier = pltpu.get_barrier_semaphore()
    for height in range(inner):
        pl.semaphore_signal(barrier, inc=1, device_id={"leaf": flipped(leaf, 1 << height)}, device_id_type=MESH)
    for mask in range(1, n_grp):
        pl.semaphore_signal(barrier, inc=1, device_id={"grp": flipped(grp, mask)}, device_id_type=MESH)

    pairs = [(matrix, panel_v), (leaf_basis, leaf_v), (leaf_tri.at[0], leaf_f)]
    pairs.append((inner_basis.at[0, 0], node_v.at[pl.ds(0, inner)]))
    pairs.append((inner_tri.at[0, 0], node_f.at[pl.ds(0, inner)]))
    pairs.append((outer_basis.at[0, 0], node_v.at[pl.ds(inner, outer)]))
    pairs.append((outer_tri.at[0, 0], node_f.at[pl.ds(inner, outer)]))
    loads = [pltpu.make_async_copy(src, dst, load_sem.at[i]) for i, (src, dst) in enumerate(pairs)]
    for load in loads[:3]:
        load.start()

    sent = []

    def send(src, dst, device):
        slot = len(sent)
        copy = pltpu.make_async_remote_copy(
            src_ref=src, dst_ref=dst, send_sem=send_sem.at[slot], recv_sem=recv_sem.at[slot],
            device_id=device, device_id_type=MESH)
        copy.start()
        sent.append(copy)
        return copy

    columns = lax.broadcasted_iota(jnp.int32, (1, panel), 1)
    half = panel // 2
    stream_rows = half // STREAMS
    width = panel // (n_leaf * n_grp)
    narrow = width // STREAMS
    owner, place = lax.div(columns, width), lax.rem(columns, width)
    target = lax.div(place, narrow) * stream_rows + lax.rem(place, narrow)
    for height in range(inner + outer):
        bit = bit_of(owner, height)
        if height < inner or scatter:
            mine = bit_of(leaf, height) if height < inner else bit_of(grp, height - inner)
            target = target + (bit + mine - 2 * bit * mine) * (stream_rows >> height if height else half)
        else:
            target = target + bit * (narrow << (height - inner))
    streams = range(STREAMS)

    def half_basis(level, parity, span=slice(None)):
        return node_v[level, pl.ds(pl.multiple_of(parity * k, k), k), span]

    rows = lax.broadcasted_iota(jnp.int32, (panel, panel), 0)
    order = jnp.where(rows == target, 1.0, 0.0).astype(BF16)
    loads[0].wait()
    turned = dot_nt(order, panel_v[...]).astype(BF16)
    for load in loads[3:]:
        load.start()
    loads[1].wait()
    projected = dot(turned, leaf_v[...])
    loads[2].wait()

    mid = k // 2
    spans = (slice(0, mid), slice(mid, k))

    def leaf_summit(rows):
        mixing = mix([projected[rows, span] for span in spans], leaf_f)
        for span in spans:
            yield turned[rows, span].astype(F32) - fold(dot_nt(mixing, leaf_v[span, :]))

    arriving = []
    for group, tile in enumerate(leaf_summit(slice(half, panel))):
        first[group] = tile
        if group == 0:
            pl.semaphore_wait(barrier, inner + n_grp - 1)
        arriving.append(send(first.at[group], first_in.at[group], {"leaf": flipped(leaf, 1)}))
    for group, tile in enumerate(leaf_summit(slice(0, half))):
        kept[group] = tile

    def project(stacked, level, parity):
        return [fold(dot(stacked, half_basis(level, parity, span))) for span in spans]

    def own_term(tiles, level):
        parity = bit_of(leaf, level)
        mixing = mix(project(join([stack(tile) for tile in tiles]), level, parity), node_f.at[level])
        for tile, span in zip(tiles, spans):
            yield jnp.where(parity == 0, tile, 0.0) - fold(dot_nt(mixing, node_v[level, span, :]))

    bits = tuple(range(1, inner))
    orders = axis_orders(bits)
    left = [[list(bits) for _ in orders] for _ in streams]
    waiting = [[None, None] for _ in streams]

    def pick(stream, group, height, side):
        return (slice(None),) * left[stream][group].index(height) + (side,)

    def send_part(stream, group, step):
        height = orders[group][step]
        waiting[stream][group] = send(
            parts[stream][group][step].at[pick(stream, group, height, 1)], parts_in[stream][group][step],
            {"leaf": flipped(leaf, 1 << height)})

    loads[3].wait()
    loads[4].wait()
    parity = bit_of(leaf, 0)
    own = project(join([stack(kept[group]) for group in range(2)]), 0, parity)
    for copy in arriving:
        copy.wait_recv()
    other = project(join([stack(first_in[group]) for group in range(2)]), 0, 1 - parity)
    mixing = mix([left_tile + right_tile for left_tile, right_tile in zip(own, other)], node_f.at[0])
    summit = [
        jnp.where(parity == 0, kept[group], first_in[group]) - fold(dot_nt(mixing, node_v[0, span, :]))
        for group, span in enumerate(spans)]
    for stream in streams:
        tiles = [tile[stream * stream_rows:(stream + 1) * stream_rows] for tile in summit]
        for level in range(1, inner - 1):
            tiles = list(own_term(tiles, level))
        for group, tile in enumerate(own_term(tiles, inner - 1)):
            parts[stream][group][0][...] = tile.reshape(parts[stream][group][0].shape)
            send_part(stream, group, 0)

    def halves(values):
        high = values.astype(BF16)
        return high, (values - high.astype(F32)).astype(BF16)

    def outer_joint(height):
        top = node_v.at[inner + height, pl.ds(0, k)]
        factor = node_f.at[inner + height]
        return halves(jnp.concatenate([
            dot_nt(factor[:mid, :], top[...]), dot_nt(factor[mid:, mid:], top[:, mid:])], axis=0))

    def outer_term(height, joint):
        parity = bit_of(grp, height)
        rows = lax.broadcasted_iota(jnp.int32, (k, k), 0)
        lane = lax.broadcasted_iota(jnp.int32, (k, k), 1)
        basis = half_basis(inner + height, parity)
        matrix = jnp.where((rows == lane) & (parity == 0), 1.0, 0.0) - (dot(basis, joint[0]) + dot(basis, joint[1]))
        outer_high[height], outer_low[height] = halves(matrix)

    def apply_outer(summit, height):
        stacked = stack(summit)
        return fold(dot(stacked, outer_high[height])) + dot(stacked[:summit.shape[0]], outer_low[height])

    sums = [[None, None] for _ in streams]
    coming = [[] for _ in streams]
    loads[5].wait()
    loads[6].wait()
    joints = []
    for step in range(len(bits)):
        for stream in streams:
            for group in range(2):
                height = orders[group][step]
                waiting[stream][group].wait_recv()
                total = parts[stream][group][step][pick(stream, group, height, 0)] + parts_in[stream][group][step][...]
                left[stream][group].remove(height)
                if step + 1 < len(bits):
                    parts[stream][group][step + 1][...] = total
                    send_part(stream, group, step + 1)
                else:
                    sums[stream][group] = total
            if step == 0 and stream == 0:
                joints = [outer_joint(height) for height in range(outer)]
                outer_term(0, joints[0])
            elif step == 0:
                for height in range(1, outer):
                    outer_term(height, joints[height])
            if step + 1 == len(bits):
                summit = jnp.concatenate(sums[stream], axis=1)
                for height in range(outer):
                    summit = apply_outer(summit, height)
                last[stream] = summit.reshape(last.shape[1:])
                for mask in range(1, n_grp):
                    piece = reversed_bits(mask, outer) if scatter else 0
                    coming[stream].append(send(
                        last.at[stream, piece], last_in.at[stream, mask - 1], {"grp": flipped(grp, mask)}))
    totals = []
    for stream in streams:
        total = last[stream, 0]
        for slot, copy in enumerate(coming[stream]):
            copy.wait_recv()
            total = total + last_in[stream, slot]
        totals.append(total)
    out[...] = jnp.concatenate(totals, axis=0).astype(out.dtype)
    for copy in sent:
        copy.wait_send()


def per_device(matrix, leaf_basis, leaf_tri, inner_basis, inner_tri, outer_basis, outer_tri):
    n_leaf, n_grp = lax.axis_size("leaf"), lax.axis_size("grp")
    panel, k = matrix.shape[1], leaf_tri.shape[-1]
    inner, outer = n_leaf.bit_length() - 1, n_grp.bit_length() - 1
    inner_rows, scatter = plan(panel, n_leaf, n_grp)
    levels = inner + outer
    rows = inner_rows // n_grp if scatter else inner_rows
    half = panel // 2
    lead = lambda count: (2,) * count + (inner_rows, k // 2)
    steps = range(inner - 1)
    parts = [[[pltpu.VMEM(lead(inner - 1 - s), F32) for s in steps] for _ in range(2)] for _ in range(STREAMS)]
    parts_in = [[[pltpu.VMEM(lead(inner - 2 - s), F32) for s in steps] for _ in range(2)] for _ in range(STREAMS)]
    copies = 2 + STREAMS * (2 * (inner - 1) + n_grp - 1)
    result = pl.pallas_call(
        functools.partial(kernel, n_leaf, n_grp),
        out_shape=jax.ShapeDtypeStruct((STREAMS * rows, k), BF16),
        in_specs=[pl.BlockSpec(memory_space=pl.ANY)] * 7,
        out_specs=pl.BlockSpec(memory_space=pltpu.VMEM),
        scratch_shapes=[
            pltpu.VMEM(matrix.shape, BF16),
            pltpu.VMEM(leaf_basis.shape, BF16),
            pltpu.VMEM(leaf_tri.shape[1:], BF16),
            pltpu.VMEM((levels,) + inner_basis.shape[-2:], BF16),
            pltpu.VMEM((levels,) + inner_tri.shape[-2:], BF16),
            pltpu.VMEM((outer, k, k), BF16),
            pltpu.VMEM((outer, k, k), BF16),
            pltpu.VMEM((2, half, k // 2), F32),
            pltpu.VMEM((2, half, k // 2), F32),
            pltpu.VMEM((2, half, k // 2), F32),
            parts,
            parts_in,
            pltpu.VMEM((STREAMS, n_grp if scatter else 1, rows, k), F32),
            pltpu.VMEM((STREAMS, n_grp - 1, rows, k), F32),
            pltpu.SemaphoreType.DMA((7,)),
            pltpu.SemaphoreType.DMA((copies,)),
            pltpu.SemaphoreType.DMA((copies,)),
        ],
        compiler_params=pltpu.CompilerParams(
            collective_id=0, has_side_effects=True, vmem_limit_bytes=60 * 2**20),
        cost_estimate=pl.CostEstimate(flops=30 * 2 * k**3, bytes_accessed=10 * 2**20, transcendentals=0),
    )(matrix, leaf_basis, leaf_tri, inner_basis, inner_tri, outer_basis, outer_tri)
    if not scatter:
        narrow = panel // (n_leaf * n_grp) // STREAMS
        result = result.reshape(STREAMS, rows, k)
        result = lax.dynamic_slice_in_dim(result, lax.axis_index("grp") * narrow, narrow, 1)
        result = result.reshape(STREAMS * narrow, k)
    return result.T


def solution(mesh):
    placed = (
        P(("grp", "leaf"), None),
        P(("grp", "leaf"), None),
        P(("grp", "leaf"), None, None),
        P("grp", "leaf", None, None, None),
        P("grp", "leaf", None, None, None),
        P("grp", "leaf", None, None, None),
        P("grp", "leaf", None, None, None),
    )
    return jax.shard_map(
        per_device, mesh=mesh, in_specs=placed, out_specs=P(None, ("grp", "leaf")), check_vma=False
    )
```

```python
import functools

import jax
import jax.numpy as jnp
from jax import lax
from jax.experimental import pallas as pl
from jax.experimental.pallas import tpu as pltpu
from jax.sharding import PartitionSpec as P

MESH = pl.DeviceIdType.MESH
F32 = jnp.float32
BF16 = jnp.bfloat16
STREAMS = 2


def dot(left, right):
    return jnp.dot(left, right, preferred_element_type=F32)


def dot_nt(left, right):
    return lax.dot_general(left, right, (((1,), (1,)), ((), ())), preferred_element_type=F32)


def stack(values):
    high = values.astype(BF16)
    low = values - high.astype(F32)
    if values.shape[0] % 16:
        return jnp.concatenate([high.astype(F32), low], axis=0).astype(BF16)
    return jnp.concatenate([high, low.astype(BF16)], axis=0)


def fold(both):
    count = both.shape[0] // 2
    return both[:count] + both[count:]


def join(tiles):
    return jnp.concatenate(tiles, axis=1)


def mix(projected, factor):
    mid = factor.shape[0] // 2
    low_tile, high_tile = [stack(tile) for tile in projected]
    first = stack(fold(dot(low_tile, factor[:mid, :mid])))
    return join([first, stack(fold(dot(join([low_tile, high_tile]), factor[:, mid:])))])


def bit_of(index, height):
    return lax.rem(lax.div(index, 2**height), 2)


def flipped(index, mask):
    for height in range(mask.bit_length()):
        if mask >> height & 1:
            index = index + 2**height * (1 - 2 * bit_of(index, height))
    return index


def reversed_bits(index, count):
    return sum((index >> i & 1) << (count - 1 - i) for i in range(count))


def plan(panel, n_leaf, n_grp):
    inner_rows = panel // n_leaf // STREAMS
    return inner_rows, inner_rows // n_grp >= 8


def axis_orders(bits):
    half = (len(bits) + 1) // 2
    return (bits, bits[half:] + bits[:half])


def kernel(n_leaf, n_grp, *refs):
    (matrix, leaf_basis, leaf_tri, inner_basis, inner_tri, outer_basis, outer_tri, out,
     panel_v, leaf_v, leaf_f, node_v, node_f, outer_high, outer_low, first, kept, first_in, parts, parts_in,
     last, last_in, load_sem, send_sem, recv_sem) = refs
    panel = matrix.shape[1]
    k = leaf_tri.shape[-1]
    inner, outer = n_leaf.bit_length() - 1, n_grp.bit_length() - 1
    inner_rows, scatter = plan(panel, n_leaf, n_grp)
    leaf, grp = lax.axis_index("leaf"), lax.axis_index("grp")

    barrier = pltpu.get_barrier_semaphore()
    for height in range(inner):
        pl.semaphore_signal(barrier, inc=1, device_id={"leaf": flipped(leaf, 1 << height)}, device_id_type=MESH)
    for mask in range(1, n_grp):
        pl.semaphore_signal(barrier, inc=1, device_id={"grp": flipped(grp, mask)}, device_id_type=MESH)

    pairs = [(matrix, panel_v), (leaf_basis, leaf_v), (leaf_tri.at[0], leaf_f)]
    for height in range(inner):
        pairs.append((inner_basis.at[0, 0, height], node_v.at[height]))
        pairs.append((inner_tri.at[0, 0, height], node_f.at[height]))
    for height in range(outer):
        pairs.append((outer_basis.at[0, 0, height], node_v.at[inner + height]))
        pairs.append((outer_tri.at[0, 0, height], node_f.at[inner + height]))
    loads = [pltpu.make_async_copy(src, dst, load_sem.at[i]) for i, (src, dst) in enumerate(pairs)]
    for load in loads:
        load.start()

    sent = []

    def send(src, dst, device):
        slot = len(sent)
        copy = pltpu.make_async_remote_copy(
            src_ref=src, dst_ref=dst, send_sem=send_sem.at[slot], recv_sem=recv_sem.at[slot],
            device_id=device, device_id_type=MESH)
        copy.start()
        sent.append(copy)
        return copy

    columns = lax.broadcasted_iota(jnp.int32, (1, panel), 1)
    half = panel // 2
    stream_rows = half // STREAMS
    width = panel // (n_leaf * n_grp)
    narrow = width // STREAMS
    owner, place = lax.div(columns, width), lax.rem(columns, width)
    target = lax.div(place, narrow) * stream_rows + lax.rem(place, narrow)
    for height in range(inner + outer):
        bit = bit_of(owner, height)
        if height < inner or scatter:
            mine = bit_of(leaf, height) if height < inner else bit_of(grp, height - inner)
            target = target + (bit + mine - 2 * bit * mine) * (stream_rows >> height if height else half)
        else:
            target = target + bit * (narrow << (height - inner))
    streams = range(STREAMS)

    def load_node(level):
        loads[3 + 2 * level].wait()
        loads[4 + 2 * level].wait()

    def half_basis(level, parity, span=slice(None)):
        return node_v[level, pl.ds(pl.multiple_of(parity * k, k), k), span]

    rows = lax.broadcasted_iota(jnp.int32, (panel, panel), 0)
    order = jnp.where(rows == target, 1.0, 0.0).astype(BF16)
    loads[0].wait()
    turned = dot_nt(order, panel_v[...]).astype(BF16)
    loads[1].wait()
    projected = dot(turned, leaf_v[...])
    loads[2].wait()

    mid = k // 2
    spans = (slice(0, mid), slice(mid, k))

    def leaf_summit(ref, rows):
        mixing = mix([projected[rows, span] for span in spans], leaf_f)
        for span in spans:
            ref[:, span] = turned[rows, span].astype(F32) - fold(dot_nt(mixing, leaf_v[span, :]))

    leaf_summit(first, slice(half, panel))
    pl.semaphore_wait(barrier, inner + n_grp - 1)
    arriving = send(first, first_in, {"leaf": flipped(leaf, 1)})
    leaf_summit(kept, slice(0, half))

    def project(stacked, level, parity):
        return [fold(dot(stacked, half_basis(level, parity, span))) for span in spans]

    def own_term(tiles, level):
        parity = bit_of(leaf, level)
        mixing = mix(project(join([stack(tile) for tile in tiles]), level, parity), node_f.at[level])
        for tile, span in zip(tiles, spans):
            yield jnp.where(parity == 0, tile, 0.0) - fold(dot_nt(mixing, node_v[level, span, :]))

    bits = tuple(range(1, inner))
    orders = axis_orders(bits)
    left = [[list(bits) for _ in orders] for _ in streams]
    waiting = [[None, None] for _ in streams]

    def pick(stream, group, height, side):
        return (slice(None),) * left[stream][group].index(height) + (side,)

    def send_part(stream, group, step):
        height = orders[group][step]
        waiting[stream][group] = send(
            parts[stream][group][step].at[pick(stream, group, height, 1)], parts_in[stream][group][step],
            {"leaf": flipped(leaf, 1 << height)})

    load_node(0)
    parity = bit_of(leaf, 0)
    own = project(stack(kept[...]), 0, parity)
    arriving.wait_recv()
    other = project(stack(first_in[...]), 0, 1 - parity)
    mixing = mix([left_tile + right_tile for left_tile, right_tile in zip(own, other)], node_f.at[0])
    summit = [
        jnp.where(parity == 0, kept[:, span], first_in[:, span]) - fold(dot_nt(mixing, node_v[0, span, :]))
        for span in spans]
    for stream in streams:
        tiles = [tile[stream * stream_rows:(stream + 1) * stream_rows] for tile in summit]
        for level in range(1, inner):
            if stream == 0:
                load_node(level)
            if level < inner - 1:
                tiles = list(own_term(tiles, level))
        for group, tile in enumerate(own_term(tiles, inner - 1)):
            parts[stream][group][0][...] = tile.reshape(parts[stream][group][0].shape)
            send_part(stream, group, 0)

    def outer_term(height):
        level, parity = inner + height, bit_of(grp, height)
        load_node(level)
        rows = lax.broadcasted_iota(jnp.int32, (k, k), 0)
        lane = lax.broadcasted_iota(jnp.int32, (k, k), 1)
        joint = jnp.concatenate([
            dot_nt(node_f[level, :mid, :], node_v[level, :k, :]),
            dot_nt(node_f[level, mid:, mid:], node_v[level, :k, mid:])], axis=0)
        high = joint.astype(BF16)
        low = (joint - high.astype(F32)).astype(BF16)
        basis = half_basis(level, parity)
        matrix = jnp.where((rows == lane) & (parity == 0), 1.0, 0.0) - (dot(basis, high) + dot(basis, low))
        high = matrix.astype(BF16)
        outer_high[height] = high
        outer_low[height] = (matrix - high.astype(F32)).astype(BF16)

    def apply_outer(summit, height):
        stacked = stack(summit)
        return fold(dot(stacked, outer_high[height])) + dot(stacked[:summit.shape[0]], outer_low[height])

    sums = [[None, None] for _ in streams]
    coming = [[] for _ in streams]
    ahead = list(range(outer))
    for step in range(len(bits)):
        for stream in streams:
            for group in range(2):
                height = orders[group][step]
                waiting[stream][group].wait_recv()
                total = parts[stream][group][step][pick(stream, group, height, 0)] + parts_in[stream][group][step][...]
                left[stream][group].remove(height)
                if step + 1 < len(bits):
                    parts[stream][group][step + 1][...] = total
                    send_part(stream, group, step + 1)
                else:
                    sums[stream][group] = total
            if ahead:
                outer_term(ahead.pop(0))
            if step + 1 == len(bits):
                summit = jnp.concatenate(sums[stream], axis=1)
                for height in range(outer):
                    summit = apply_outer(summit, height)
                last[stream] = summit.reshape(last.shape[1:])
                for mask in range(1, n_grp):
                    piece = reversed_bits(mask, outer) if scatter else 0
                    coming[stream].append(send(
                        last.at[stream, piece], last_in.at[stream, mask - 1], {"grp": flipped(grp, mask)}))
    totals = []
    for stream in streams:
        total = last[stream, 0]
        for slot, copy in enumerate(coming[stream]):
            copy.wait_recv()
            total = total + last_in[stream, slot]
        totals.append(total)
    out[...] = jnp.concatenate(totals, axis=0).astype(out.dtype)
    for copy in sent:
        copy.wait_send()


def per_device(matrix, leaf_basis, leaf_tri, inner_basis, inner_tri, outer_basis, outer_tri):
    n_leaf, n_grp = lax.axis_size("leaf"), lax.axis_size("grp")
    panel, k = matrix.shape[1], leaf_tri.shape[-1]
    inner, outer = n_leaf.bit_length() - 1, n_grp.bit_length() - 1
    inner_rows, scatter = plan(panel, n_leaf, n_grp)
    levels = inner + outer
    rows = inner_rows // n_grp if scatter else inner_rows
    half = panel // 2
    lead = lambda count: (2,) * count + (inner_rows, k // 2)
    steps = range(inner - 1)
    parts = [[[pltpu.VMEM(lead(inner - 1 - s), F32) for s in steps] for _ in range(2)] for _ in range(STREAMS)]
    parts_in = [[[pltpu.VMEM(lead(inner - 2 - s), F32) for s in steps] for _ in range(2)] for _ in range(STREAMS)]
    copies = 1 + STREAMS * (2 * (inner - 1) + n_grp - 1)
    result = pl.pallas_call(
        functools.partial(kernel, n_leaf, n_grp),
        out_shape=jax.ShapeDtypeStruct((STREAMS * rows, k), BF16),
        in_specs=[pl.BlockSpec(memory_space=pl.ANY)] * 7,
        out_specs=pl.BlockSpec(memory_space=pltpu.VMEM),
        scratch_shapes=[
            pltpu.VMEM(matrix.shape, BF16),
            pltpu.VMEM(leaf_basis.shape, BF16),
            pltpu.VMEM(leaf_tri.shape[1:], BF16),
            pltpu.VMEM((levels,) + inner_basis.shape[-2:], BF16),
            pltpu.VMEM((levels,) + inner_tri.shape[-2:], BF16),
            pltpu.VMEM((outer, k, k), BF16),
            pltpu.VMEM((outer, k, k), BF16),
            pltpu.VMEM((half, k), F32),
            pltpu.VMEM((half, k), F32),
            pltpu.VMEM((half, k), F32),
            parts,
            parts_in,
            pltpu.VMEM((STREAMS, n_grp if scatter else 1, rows, k), F32),
            pltpu.VMEM((STREAMS, n_grp - 1, rows, k), F32),
            pltpu.SemaphoreType.DMA((3 + 2 * levels,)),
            pltpu.SemaphoreType.DMA((copies,)),
            pltpu.SemaphoreType.DMA((copies,)),
        ],
        compiler_params=pltpu.CompilerParams(
            collective_id=0, has_side_effects=True, vmem_limit_bytes=60 * 2**20),
        cost_estimate=pl.CostEstimate(flops=30 * 2 * k**3, bytes_accessed=10 * 2**20, transcendentals=0),
    )(matrix, leaf_basis, leaf_tri, inner_basis, inner_tri, outer_basis, outer_tri)
    if not scatter:
        narrow = panel // (n_leaf * n_grp) // STREAMS
        result = result.reshape(STREAMS, rows, k)
        result = lax.dynamic_slice_in_dim(result, lax.axis_index("grp") * narrow, narrow, 1)
        result = result.reshape(STREAMS * narrow, k)
    return result.T


def solution(mesh):
    placed = (
        P(("grp", "leaf"), None),
        P(("grp", "leaf"), None),
        P(("grp", "leaf"), None, None),
        P("grp", "leaf", None, None, None),
        P("grp", "leaf", None, None, None),
        P("grp", "leaf", None, None, None),
        P("grp", "leaf", None, None, None),
    )
    return jax.shard_map(
        per_device, mesh=mesh, in_specs=placed, out_specs=P(None, ("grp", "leaf")), check_vma=False
    )
```

```python
import functools

import jax
import jax.numpy as jnp
from jax import lax
from jax.experimental import pallas as pl
from jax.experimental.pallas import tpu as pltpu
from jax.sharding import PartitionSpec as P

MESH = pl.DeviceIdType.MESH
F32 = jnp.float32
BF16 = jnp.bfloat16
STREAMS = 2


def dot(left, right):
    return jnp.dot(left, right, preferred_element_type=F32)


def dot_nt(left, right):
    return lax.dot_general(left, right, (((1,), (1,)), ((), ())), preferred_element_type=F32)


def stack(values):
    high = values.astype(BF16)
    low = values - high.astype(F32)
    if values.shape[0] % 16:
        return jnp.concatenate([high.astype(F32), low], axis=0).astype(BF16)
    return jnp.concatenate([high, low.astype(BF16)], axis=0)


def fold(both):
    count = both.shape[0] // 2
    return both[:count] + both[count:]


def join(tiles):
    return jnp.concatenate(tiles, axis=1)


def mix(projected, factor):
    mid = factor.shape[0] // 2
    low_tile, high_tile = [stack(tile) for tile in projected]
    first = stack(fold(dot(low_tile, factor[:mid, :mid])))
    return join([first, stack(fold(dot(join([low_tile, high_tile]), factor[:, mid:])))])


def bit_of(index, height):
    return lax.rem(lax.div(index, 2**height), 2)


def flipped(index, mask):
    for height in range(mask.bit_length()):
        if mask >> height & 1:
            index = index + 2**height * (1 - 2 * bit_of(index, height))
    return index


def reversed_bits(index, count):
    return sum((index >> i & 1) << (count - 1 - i) for i in range(count))


def plan(panel, n_leaf, n_grp):
    inner_rows = panel // n_leaf // STREAMS
    return inner_rows, inner_rows // n_grp >= 8


def axis_orders(bits):
    half = (len(bits) + 1) // 2
    return (bits, bits[half:] + bits[:half])


def kernel(n_leaf, n_grp, *refs):
    (matrix, leaf_basis, leaf_tri, inner_basis, inner_tri, outer_basis, outer_tri, out,
     panel_v, leaf_v, leaf_f, node_v, node_f, outer_high, outer_low, first, kept, first_in, parts, parts_in,
     last, last_in, load_sem, send_sem, recv_sem) = refs
    panel = matrix.shape[1]
    k = leaf_tri.shape[-1]
    inner, outer = n_leaf.bit_length() - 1, n_grp.bit_length() - 1
    inner_rows, scatter = plan(panel, n_leaf, n_grp)
    leaf, grp = lax.axis_index("leaf"), lax.axis_index("grp")

    barrier = pltpu.get_barrier_semaphore()
    for height in range(inner):
        pl.semaphore_signal(barrier, inc=1, device_id={"leaf": flipped(leaf, 1 << height)}, device_id_type=MESH)
    for mask in range(1, n_grp):
        pl.semaphore_signal(barrier, inc=1, device_id={"grp": flipped(grp, mask)}, device_id_type=MESH)

    pairs = [(matrix, panel_v), (leaf_basis, leaf_v), (leaf_tri.at[0], leaf_f)]
    for height in range(inner):
        pairs.append((inner_basis.at[0, 0, height], node_v.at[height]))
        pairs.append((inner_tri.at[0, 0, height], node_f.at[height]))
    for height in range(outer):
        pairs.append((outer_basis.at[0, 0, height], node_v.at[inner + height]))
        pairs.append((outer_tri.at[0, 0, height], node_f.at[inner + height]))
    loads = [pltpu.make_async_copy(src, dst, load_sem.at[i]) for i, (src, dst) in enumerate(pairs)]
    for load in loads[:3]:
        load.start()

    sent = []

    def send(src, dst, device):
        slot = len(sent)
        copy = pltpu.make_async_remote_copy(
            src_ref=src, dst_ref=dst, send_sem=send_sem.at[slot], recv_sem=recv_sem.at[slot],
            device_id=device, device_id_type=MESH)
        copy.start()
        sent.append(copy)
        return copy

    columns = lax.broadcasted_iota(jnp.int32, (1, panel), 1)
    half = panel // 2
    stream_rows = half // STREAMS
    width = panel // (n_leaf * n_grp)
    narrow = width // STREAMS
    owner, place = lax.div(columns, width), lax.rem(columns, width)
    target = lax.div(place, narrow) * stream_rows + lax.rem(place, narrow)
    for height in range(inner + outer):
        bit = bit_of(owner, height)
        if height < inner or scatter:
            mine = bit_of(leaf, height) if height < inner else bit_of(grp, height - inner)
            target = target + (bit + mine - 2 * bit * mine) * (stream_rows >> height if height else half)
        else:
            target = target + bit * (narrow << (height - inner))
    streams = range(STREAMS)

    def load_node(level):
        loads[3 + 2 * level].wait()
        loads[4 + 2 * level].wait()

    def half_basis(level, parity, span=slice(None)):
        return node_v[level, pl.ds(pl.multiple_of(parity * k, k), k), span]

    mid = k // 2
    spans = (slice(0, mid), slice(mid, k))

    def leaf_order(start):
        rows = lax.broadcasted_iota(jnp.int32, (half, panel), 0) + start
        return jnp.where(rows == target, 1.0, 0.0).astype(BF16)

    def leaf_tiles(turned, projected):
        mixing = mix([projected[:, span] for span in spans], leaf_f)
        for span in spans:
            yield turned[:, span].astype(F32) - fold(dot_nt(mixing, leaf_v[span, :]))

    order = leaf_order(half)
    loads[0].wait()
    turned = dot_nt(order, panel_v[...]).astype(BF16)
    loads[1].wait()
    loads[2].wait()
    for load in loads[3:]:
        load.start()
    arriving = []
    for group, tile in enumerate(leaf_tiles(turned, dot(turned, leaf_v[...]))):
        first[group] = tile
        if group == 0:
            pl.semaphore_wait(barrier, inner + n_grp - 1)
        arriving.append(send(first.at[group], first_in.at[group], {"leaf": flipped(leaf, 1)}))
    turned = dot_nt(leaf_order(0), panel_v[...]).astype(BF16)
    for group, tile in enumerate(leaf_tiles(turned, dot(turned, leaf_v[...]))):
        kept[group] = tile

    def project(stacked, level, parity):
        return [fold(dot(stacked, half_basis(level, parity, span))) for span in spans]

    def own_term(tiles, level):
        parity = bit_of(leaf, level)
        mixing = mix(project(join([stack(tile) for tile in tiles]), level, parity), node_f.at[level])
        for tile, span in zip(tiles, spans):
            yield jnp.where(parity == 0, tile, 0.0) - fold(dot_nt(mixing, node_v[level, span, :]))

    bits = tuple(range(1, inner))
    orders = axis_orders(bits)
    left = [[list(bits) for _ in orders] for _ in streams]
    waiting = [[None, None] for _ in streams]

    def pick(stream, group, height, side):
        return (slice(None),) * left[stream][group].index(height) + (side,)

    def send_part(stream, group, step):
        height = orders[group][step]
        waiting[stream][group] = send(
            parts[stream][group][step].at[pick(stream, group, height, 1)], parts_in[stream][group][step],
            {"leaf": flipped(leaf, 1 << height)})

    for level in range(inner):
        load_node(level)
    parity = bit_of(leaf, 0)
    own = project(join([stack(kept[group]) for group in range(2)]), 0, parity)
    for copy in arriving:
        copy.wait_recv()
    other = project(join([stack(first_in[group]) for group in range(2)]), 0, 1 - parity)
    mixing = mix([left_tile + right_tile for left_tile, right_tile in zip(own, other)], node_f.at[0])
    summit = [
        jnp.where(parity == 0, kept[group], first_in[group]) - fold(dot_nt(mixing, node_v[0, span, :]))
        for group, span in enumerate(spans)]
    for stream in streams:
        tiles = [tile[stream * stream_rows:(stream + 1) * stream_rows] for tile in summit]
        for level in range(1, inner - 1):
            tiles = list(own_term(tiles, level))
        for group, tile in enumerate(own_term(tiles, inner - 1)):
            parts[stream][group][0][...] = tile.reshape(parts[stream][group][0].shape)
            send_part(stream, group, 0)

    def outer_term(height):
        level, parity = inner + height, bit_of(grp, height)
        load_node(level)
        rows = lax.broadcasted_iota(jnp.int32, (k, k), 0)
        lane = lax.broadcasted_iota(jnp.int32, (k, k), 1)
        joint = jnp.concatenate([
            dot_nt(node_f[level, :mid, :], node_v[level, :k, :]),
            dot_nt(node_f[level, mid:, mid:], node_v[level, :k, mid:])], axis=0)
        high = joint.astype(BF16)
        low = (joint - high.astype(F32)).astype(BF16)
        basis = half_basis(level, parity)
        matrix = jnp.where((rows == lane) & (parity == 0), 1.0, 0.0) - (dot(basis, high) + dot(basis, low))
        high = matrix.astype(BF16)
        outer_high[height] = high
        outer_low[height] = (matrix - high.astype(F32)).astype(BF16)

    def apply_outer(summit, height):
        stacked = stack(summit)
        return fold(dot(stacked, outer_high[height])) + dot(stacked[:summit.shape[0]], outer_low[height])

    sums = [[None, None] for _ in streams]
    coming = [[] for _ in streams]
    ahead = list(range(outer))
    for step in range(len(bits)):
        for stream in streams:
            for group in range(2):
                height = orders[group][step]
                waiting[stream][group].wait_recv()
                total = parts[stream][group][step][pick(stream, group, height, 0)] + parts_in[stream][group][step][...]
                left[stream][group].remove(height)
                if step + 1 < len(bits):
                    parts[stream][group][step + 1][...] = total
                    send_part(stream, group, step + 1)
                else:
                    sums[stream][group] = total
            if ahead:
                outer_term(ahead.pop(0))
            if step + 1 == len(bits):
                summit = jnp.concatenate(sums[stream], axis=1)
                for height in range(outer):
                    summit = apply_outer(summit, height)
                last[stream] = summit.reshape(last.shape[1:])
                for mask in range(1, n_grp):
                    piece = reversed_bits(mask, outer) if scatter else 0
                    coming[stream].append(send(
                        last.at[stream, piece], last_in.at[stream, mask - 1], {"grp": flipped(grp, mask)}))
    totals = []
    for stream in streams:
        total = last[stream, 0]
        for slot, copy in enumerate(coming[stream]):
            copy.wait_recv()
            total = total + last_in[stream, slot]
        totals.append(total)
    out[...] = jnp.concatenate(totals, axis=0).astype(out.dtype)
    for copy in sent:
        copy.wait_send()


def per_device(matrix, leaf_basis, leaf_tri, inner_basis, inner_tri, outer_basis, outer_tri):
    n_leaf, n_grp = lax.axis_size("leaf"), lax.axis_size("grp")
    panel, k = matrix.shape[1], leaf_tri.shape[-1]
    inner, outer = n_leaf.bit_length() - 1, n_grp.bit_length() - 1
    inner_rows, scatter = plan(panel, n_leaf, n_grp)
    levels = inner + outer
    rows = inner_rows // n_grp if scatter else inner_rows
    half = panel // 2
    lead = lambda count: (2,) * count + (inner_rows, k // 2)
    steps = range(inner - 1)
    parts = [[[pltpu.VMEM(lead(inner - 1 - s), F32) for s in steps] for _ in range(2)] for _ in range(STREAMS)]
    parts_in = [[[pltpu.VMEM(lead(inner - 2 - s), F32) for s in steps] for _ in range(2)] for _ in range(STREAMS)]
    copies = 2 + STREAMS * (2 * (inner - 1) + n_grp - 1)
    result = pl.pallas_call(
        functools.partial(kernel, n_leaf, n_grp),
        out_shape=jax.ShapeDtypeStruct((STREAMS * rows, k), BF16),
        in_specs=[pl.BlockSpec(memory_space=pl.ANY)] * 7,
        out_specs=pl.BlockSpec(memory_space=pltpu.VMEM),
        scratch_shapes=[
            pltpu.VMEM(matrix.shape, BF16),
            pltpu.VMEM(leaf_basis.shape, BF16),
            pltpu.VMEM(leaf_tri.shape[1:], BF16),
            pltpu.VMEM((levels,) + inner_basis.shape[-2:], BF16),
            pltpu.VMEM((levels,) + inner_tri.shape[-2:], BF16),
            pltpu.VMEM((outer, k, k), BF16),
            pltpu.VMEM((outer, k, k), BF16),
            pltpu.VMEM((2, half, k // 2), F32),
            pltpu.VMEM((2, half, k // 2), F32),
            pltpu.VMEM((2, half, k // 2), F32),
            parts,
            parts_in,
            pltpu.VMEM((STREAMS, n_grp if scatter else 1, rows, k), F32),
            pltpu.VMEM((STREAMS, n_grp - 1, rows, k), F32),
            pltpu.SemaphoreType.DMA((3 + 2 * levels,)),
            pltpu.SemaphoreType.DMA((copies,)),
            pltpu.SemaphoreType.DMA((copies,)),
        ],
        compiler_params=pltpu.CompilerParams(
            collective_id=0, has_side_effects=True, vmem_limit_bytes=60 * 2**20),
        cost_estimate=pl.CostEstimate(flops=30 * 2 * k**3, bytes_accessed=10 * 2**20, transcendentals=0),
    )(matrix, leaf_basis, leaf_tri, inner_basis, inner_tri, outer_basis, outer_tri)
    if not scatter:
        narrow = panel // (n_leaf * n_grp) // STREAMS
        result = result.reshape(STREAMS, rows, k)
        result = lax.dynamic_slice_in_dim(result, lax.axis_index("grp") * narrow, narrow, 1)
        result = result.reshape(STREAMS * narrow, k)
    return result.T


def solution(mesh):
    placed = (
        P(("grp", "leaf"), None),
        P(("grp", "leaf"), None),
        P(("grp", "leaf"), None, None),
        P("grp", "leaf", None, None, None),
        P("grp", "leaf", None, None, None),
        P("grp", "leaf", None, None, None),
        P("grp", "leaf", None, None, None),
    )
    return jax.shard_map(
        per_device, mesh=mesh, in_specs=placed, out_specs=P(None, ("grp", "leaf")), check_vma=False
    )
```
